32 devices in a mesh: dp: 2 (over x), expert: 4 (over y, core), tensor: 4 (over z).
Axes of the slice: x: 2, y: 2, z: 4, core: 2. Of those that a mesh axis runs over, the one named last changes fastest.
Arguments:
- layer_input: bfloat16 [2, 2048, 2048], P('dp', 'expert'), may hold values from -6 to 6
- attention_gain: bfloat16 [2048], replicated, may hold values from 0.25 to 1.75
- query_weight: bfloat16 [2048, 2048], P(('dp', 'expert'), 'tensor'), may hold values from -0.125 to 0.125
- key_weight: bfloat16 [2048, 2048], P(('dp', 'expert'), 'tensor'), may hold values from -0.125 to 0.125
- value_weight: bfloat16 [2048, 2048], P(('dp', 'expert'), 'tensor'), may hold values from -0.125 to 0.125
- query_bias: bfloat16 [2048], P('tensor'), may hold values from -0.59765625 to 0.59765625
- key_bias: bfloat16 [2048], P('tensor'), may hold values from -0.59765625 to 0.59765625
- value_bias: bfloat16 [2048], P('tensor'), may hold values from -0.59765625 to 0.59765625
- output_weight: bfloat16 [2048, 2048], P(('dp', 'expert'), 'tensor'), may hold values from -1 to 1
- mixture_gain: bfloat16 [2048], replicated, may hold values from 0.25 to 1.75
- router_weight: bfloat16 [2048, 8], replicated, may hold values from -0.0625 to 0.0625
- expert_gate: bfloat16 [8, 2048, 1408], P('expert', None, 'tensor'), may hold values from -0.125 to 0.125
- expert_up: bfloat16 [8, 2048, 1408], P('expert', None, 'tensor'), may hold values from -0.125 to 0.125
- expert_down: bfloat16 [8, 2048, 1408], P('expert', None, 'tensor'), may hold values from -1 to 1
- shared_gate: bfloat16 [2048, 5632], P(('dp', 'expert'), 'tensor'), may hold values from -0.125 to 0.125
- shared_up: bfloat16 [2048, 5632], P(('dp', 'expert'), 'tensor'), may hold values from -0.125 to 0.125
- shared_down: bfloat16 [2048, 5632], P(('dp', 'expert'), 'tensor'), may hold values from -0.21875 to 0.21875
- shared_switch: bfloat16 [2048], replicated, may hold values from -0.125 to 0.125
- slot_lengths: int32 [2], P('dp'), may hold values from 512 to 2048, as said below
- routes: int32 [2, 2048, 4], P('dp', 'expert'), may hold values from 0 to 7, all different within a row
- cotangent: bfloat16 [2, 2048, 2048], P('dp', 'expert'), may hold values from -6 to 6
Outputs:
- layer_output: bfloat16 [2, 2048, 2048], P('dp', 'expert')
- input_grad: float32 [2, 2048, 2048], P('dp', 'expert')
- attention_gain_grad: float32 [2048], replicated
- query_weight_grad: float32 [2048, 2048], P(('dp', 'expert'), 'tensor')
- key_weight_grad: float32 [2048, 2048], P(('dp', 'expert'), 'tensor')
- value_weight_grad: float32 [2048, 2048], P(('dp', 'expert'), 'tensor')
- query_bias_grad: float32 [2048], P('tensor')
- key_bias_grad: float32 [2048], P('tensor')
- value_bias_grad: float32 [2048], P('tensor')
- output_weight_grad: float32 [2048, 2048], P(('dp', 'expert'), 'tensor')
- mixture_gain_grad: float32 [2048], replicated
- router_weight_grad: float32 [2048, 8], replicated
- expert_gate_grad: float32 [8, 2048, 1408], P('expert', None, 'tensor')
- expert_up_grad: float32 [8, 2048, 1408], P('expert', None, 'tensor')
- expert_down_grad: float32 [8, 2048, 1408], P('expert', None, 'tensor')
- shared_gate_grad: float32 [2048, 5632], P(('dp', 'expert'), 'tensor')
- shared_up_grad: float32 [2048, 5632], P(('dp', 'expert'), 'tensor')
- shared_down_grad: float32 [2048, 5632], P(('dp', 'expert'), 'tensor')
- shared_switch_grad: float32 [2048], replicated
The draws below stay inside these ranges and needn't reach their ends.
Inputs may be any that keep to these rules, and one draw needn't show every extreme that they name: `slot_lengths`: one slot has exactly 2048 valid tokens.
All inputs are finite; a program needn't handle non-finite values.
Results may differ from the reference program's by a relative error of at most 0.02.
Values may be sent and summed in bfloat16 or wider, within the bound.
No kernel may reach another device: no remote copies, remote signals or barrier semaphores. Data moves between devices by JAX's collectives and lax.ppermute only.
A program may use at most 320 MiB of HBM per device.

```python
import jax
import jax.numpy as jnp
from jax import lax

D = 2048
HEADS = 16
HD = 128
HQ = 2048
FE = 1408
FS = 5632
TOP = 4
EXPERTS = 8
LEN = 2048
ROWS = 512
CAP = 256
SLOTS = 2


def draw_slot_lengths(key, part):
    fresh = jax.random.randint(jax.random.fold_in(key, 11), (SLOTS,), LEN // 4, LEN + 1, dtype=jnp.int32)
    full_slot = jax.random.randint(jax.random.fold_in(key, 23), (), 0, SLOTS, dtype=jnp.int32)
    slot_ids = jnp.arange(SLOTS, dtype=jnp.int32)
    return jnp.where(slot_ids == full_slot, jnp.int32(LEN), fresh).astype(jnp.int32)


def levels(key, shape, cuts, low, top_value):
    loudness, own = 1.0, jax.random.fold_in(key, 6)
    for axis_at, shards_of in cuts:
        steps = jnp.exp(jax.random.uniform(jax.random.fold_in(own, axis_at), (shards_of,), jnp.float32, low / len(cuts), top_value / len(cuts)))
        loudness = loudness * jnp.repeat(steps, shape[axis_at] // shards_of).reshape([-1 if axis == axis_at else 1 for axis in range(len(shape))])
    return loudness


def distinct(stream_key, rows, count, top, lift):
    sequence = jax.random.permutation(jax.random.fold_in(stream_key, 1), count)
    pull = sequence
    for power in range(3):
        pull = pull * pull // count
    pull = pull * lift // count
    chance = jax.random.randint(jax.random.fold_in(stream_key, 2), (rows, count), 0, 4096) + pull
    fixed_rows = jax.random.permutation(jax.random.fold_in(stream_key, 3), rows)[jnp.arange(count) % rows]
    chance = jnp.where(jnp.arange(rows)[:, None] == fixed_rows[None, :], 1 << 14, chance)
    priority = chance * count + jnp.arange(count)
    return lax.top_k(priority.astype(jnp.int32), top)[1].astype(jnp.int32)


def bell_draw(rng, shape, scale, most, split=(), kind=jnp.bfloat16):
    entries = scale * jax.random.normal(rng, shape, jnp.float32)
    if split:
        entries = entries * levels(rng, shape, split, -0.22, 0.18)
    return jnp.clip(entries, -most, most).astype(kind)


def setup_inputs(seed: int = 0) -> dict:
    seeds = jax.random.split(jax.random.key(seed), 22)
    return {
        "layer_input": bell_draw(seeds[0], (SLOTS, LEN, D), 1.0, 6.0, ((0, 2), (1, 4))),
        "attention_gain": jnp.clip(1.0 + 0.15 * jax.random.normal(seeds[1], (D,), jnp.float32), 0.25, 1.75).astype(jnp.bfloat16),
        "query_weight": bell_draw(seeds[2], (D, HQ), D ** -0.5, 0.125, ((0, 8), (1, 4))),
        "key_weight": bell_draw(seeds[3], (D, HQ), D ** -0.5, 0.125, ((0, 8), (1, 4))),
        "value_weight": bell_draw(seeds[4], (D, HQ), D ** -0.5, 0.125, ((0, 8), (1, 4))),
        "query_bias": bell_draw(seeds[5], (HQ,), 0.1, 0.59765625, ((0, 4),)),
        "key_bias": bell_draw(seeds[6], (HQ,), 0.1, 0.59765625, ((0, 4),)),
        "value_bias": bell_draw(seeds[7], (HQ,), 0.1, 0.59765625, ((0, 4),)),
        "output_weight": bell_draw(seeds[8], (D, HQ), (HEADS * HD // 64) ** -0.5, 1.0, ((0, 8), (1, 4))),
        "mixture_gain": jnp.clip(1.0 + 0.15 * jax.random.normal(seeds[9], (D,), jnp.float32), 0.25, 1.75).astype(jnp.bfloat16),
        "router_weight": bell_draw(seeds[10], (D, EXPERTS), (4 * D) ** -0.5, 0.0625),
        "expert_gate": bell_draw(seeds[11], (EXPERTS, D, FE), D ** -0.5, 0.125, ((0, 4), (2, 4))),
        "expert_up": bell_draw(seeds[12], (EXPERTS, D, FE), D ** -0.5, 0.125, ((0, 4), (2, 4))),
        "expert_down": bell_draw(seeds[13], (EXPERTS, D, FE), (max(1, TOP * FE // (3 * EXPERTS * EXPERTS))) ** -0.5, 1.0, ((0, 4), (2, 4))),
        "shared_gate": bell_draw(seeds[14], (D, FS), D ** -0.5, 0.125, ((0, 8), (1, 4))),
        "shared_up": bell_draw(seeds[15], (D, FS), D ** -0.5, 0.125, ((0, 8), (1, 4))),
        "shared_down": bell_draw(seeds[16], (D, FS), (FS // 8) ** -0.5, 0.21875, ((0, 8), (1, 4))),
        "shared_switch": bell_draw(seeds[17], (D,), D ** -0.5, 0.125),
        "slot_lengths": draw_slot_lengths(jax.random.fold_in(seeds[21], 71), 0),
        "routes": distinct(seeds[19], SLOTS * LEN, EXPERTS, TOP, 4096).reshape((SLOTS, LEN, TOP)),
        "cotangent": bell_draw(seeds[20], (SLOTS, LEN, D), 1.0, 6.0, ((0, 2), (1, 4))),
    }


@jax.custom_vjp
def low(v):
    return lax.optimization_barrier(v.astype(jnp.bfloat16)).astype(jnp.float32)

@jax.custom_vjp
def low_back(v):
    return v

def low_keep(v):
    return (low(v), None)

def low_pass(kept, grad):
    return (grad,)

def back_keep(v):
    return (v, None)

def back_low(kept, grad):
    return (low(grad),)
low.defvjp(low_keep, low_pass)
low_back.defvjp(back_keep, back_low)
EPS = 1e-06
ROPE_BASE = 1000000.0
NEGATIVE = -1e+30
PRECISE = lax.Precision.HIGHEST

def rms_scale(values, gain):
    return values * lax.rsqrt(lax.optimization_barrier(jnp.mean(values * values, axis=-1, keepdims=True)) + EPS) * gain

def softmax_rows(values):
    lifted = jnp.exp(values - lax.optimization_barrier(jnp.max(values, axis=-1, keepdims=True)))
    return lifted / lax.optimization_barrier(jnp.sum(lifted, axis=-1, keepdims=True))

def rotary_tables(positions, head_size):
    half_size = head_size // 2
    exponent = 2.0 * jnp.arange(half_size, dtype=jnp.float32) / head_size
    inverse = ROPE_BASE ** (-exponent)
    angles = positions.astype(jnp.float32)[:, None] * inverse[None, :]
    cosine_half = jnp.cos(angles)
    sine_half = jnp.sin(angles)
    return (jnp.concatenate([cosine_half, cosine_half], axis=1), jnp.concatenate([sine_half, sine_half], axis=1))

def rotate(values, cosine_table, sine_table):
    half_size = values.shape[-1] // 2
    first_half = values[..., :half_size]
    second_half = values[..., half_size:]
    turned = jnp.concatenate([-second_half, first_half], axis=-1)
    return values * cosine_table + turned * sine_table

def capacity_tables(route_block, live_block, experts, capacity):
    rows_here = route_block.shape[0]
    picks = route_block.shape[1]
    chosen = (route_block[:, :, None] == jnp.arange(experts, dtype=jnp.int32)[None, None, :]) & live_block[:, None, None]
    counts = chosen.astype(jnp.int32).reshape(rows_here * picks, experts)
    before = (jnp.cumsum(counts, axis=0, dtype=jnp.int32) - counts).astype(jnp.int32)
    place = lax.optimization_barrier(jnp.sum(before * counts, axis=1, dtype=jnp.int32)).astype(jnp.int32).reshape(rows_here, picks)
    kept = live_block[:, None] & (place < capacity)
    flat = jnp.where(kept, route_block * capacity + place, experts * capacity).astype(jnp.int32)
    row_ids = jnp.broadcast_to(jnp.arange(rows_here, dtype=jnp.int32)[:, None], (rows_here, picks))
    table = jnp.full((experts * capacity,), rows_here, jnp.int32).at[flat.reshape(-1)].set(row_ids.reshape(-1), mode='drop')
    return (kept, flat, table)

def take_rows(source, index):
    return jnp.take(source, index, axis=0, mode='fill', fill_value=0.0)

def slot_forward(slot_input, live_rows, route_slot, params):
    attention_gain, query_weight, key_weight, value_weight, query_bias, key_bias, value_bias, output_weight, mixture_gain, router_weight, expert_gate, expert_up, expert_down, shared_gate, shared_up, shared_down, shared_switch = params
    positions = jnp.arange(LEN, dtype=jnp.int32)
    cosine_table, sine_table = rotary_tables(positions, HD)
    cosine_table = cosine_table[:, None, :]
    sine_table = sine_table[:, None, :]
    normed = low(rms_scale(slot_input, attention_gain))
    query_pre = low_back(jnp.dot(normed, query_weight, precision=PRECISE) + query_bias)
    key_pre = low_back(jnp.dot(normed, key_weight, precision=PRECISE) + key_bias)
    value_low = low(low_back(jnp.dot(normed, value_weight, precision=PRECISE) + value_bias))
    query_heads = low(rotate(query_pre.reshape(LEN, HEADS, HD), cosine_table, sine_table)).transpose(1, 0, 2)
    key_heads = low(rotate(key_pre.reshape(LEN, HEADS, HD), cosine_table, sine_table)).transpose(1, 0, 2)
    value_heads = value_low.reshape(LEN, HEADS, HD).transpose(1, 0, 2)
    allowed = (positions[None, :] <= positions[:, None]) & live_rows[None, :]
    score_scale = HD ** (-0.5)

    def attend(operands):
        query_head, key_head, value_head = operands
        scores = low_back(jnp.dot(query_head, key_head.T, precision=PRECISE) * score_scale)
        weights = softmax_rows(jnp.where(allowed, scores, NEGATIVE))
        return low(low_back(jnp.dot(low(weights), value_head, precision=PRECISE)))
    head_out = lax.map(jax.checkpoint(attend), (query_heads, key_heads, value_heads))
    heads_flat = head_out.transpose(1, 0, 2).reshape(LEN, HEADS * HD)
    attended = low_back(jnp.dot(heads_flat, output_weight.T, precision=PRECISE))
    residual = slot_input + attended
    mix_in = low(rms_scale(residual, mixture_gain))
    logits = low_back(jnp.dot(mix_in, router_weight, precision=PRECISE))
    router_probs = softmax_rows(logits)
    gates = jnp.take_along_axis(router_probs, route_slot, axis=1)
    gate_lin = low_back(jnp.dot(mix_in, shared_gate, precision=PRECISE))
    up_lin = low_back(jnp.dot(mix_in, shared_up, precision=PRECISE))
    shared_hidden = low(jax.nn.silu(gate_lin) * up_lin)
    shared_out = low_back(jnp.dot(shared_hidden, shared_down.T, precision=PRECISE))
    switch = jax.nn.sigmoid(low_back(jnp.dot(mix_in, shared_switch, precision=PRECISE)))
    blocks = LEN // ROWS

    def block_tables(route_block, live_block):
        return capacity_tables(route_block, live_block, EXPERTS, CAP)
    kept, flat, table = jax.vmap(block_tables)(route_slot.reshape(blocks, ROWS, TOP), live_rows.reshape(blocks, ROWS))
    buffers = jax.vmap(take_rows)(mix_in.reshape(blocks, ROWS, D), table).reshape(blocks, EXPERTS, CAP, D)
    expert_gate_lin = low_back(jnp.einsum('becd,edf->becf', buffers, expert_gate, precision=PRECISE))
    expert_up_lin = low_back(jnp.einsum('becd,edf->becf', buffers, expert_up, precision=PRECISE))
    expert_hidden = low(jax.nn.silu(expert_gate_lin) * expert_up_lin)
    results = low_back(jnp.einsum('becf,edf->becd', expert_hidden, expert_down, precision=PRECISE))
    pairs = jax.vmap(take_rows)(results.reshape(blocks, EXPERTS * CAP, D), flat.reshape(blocks, ROWS * TOP))
    pairs = pairs.reshape(LEN, TOP, D)
    mixture = switch[:, None] * shared_out + lax.optimization_barrier(jnp.sum(gates[:, :, None] * pairs, axis=1))
    return jnp.where(live_rows[:, None], residual + mixture, 0.0)

def reference(layer_input, attention_gain, query_weight, key_weight, value_weight, query_bias, key_bias, value_bias, output_weight, mixture_gain, router_weight, expert_gate, expert_up, expert_down, shared_gate, shared_up, shared_down, shared_switch, slot_lengths, routes, cotangent):
    params = tuple((weight.astype(jnp.float32) for weight in (attention_gain, query_weight, key_weight, value_weight, query_bias, key_bias, value_bias, output_weight, mixture_gain, router_weight, expert_gate, expert_up, expert_down, shared_gate, shared_up, shared_down, shared_switch)))

    def per_slot(totals, slot_items):
        slot_input, length, route_slot, slot_cotangent = slot_items
        live_rows = jnp.arange(LEN, dtype=jnp.int32) < length

        def forward(inputs, weights):
            return slot_forward(inputs, live_rows, route_slot, weights)
        output, pullback = jax.vjp(forward, slot_input.astype(jnp.float32), params)
        input_grad, weight_grads = pullback(slot_cotangent.astype(jnp.float32))
        totals = jax.tree.map(lambda before_sum, new_term: before_sum + new_term, totals, weight_grads)
        return (totals, (output.astype(jnp.bfloat16), input_grad))
    zero_grads = jax.tree.map(jnp.zeros_like, params)
    totals, (outputs, input_grads) = lax.scan(per_slot, zero_grads, (layer_input, slot_lengths, routes, cotangent))
    return (outputs, input_grads, totals[0], totals[1], totals[2], totals[3], totals[4], totals[5], totals[6], totals[7], totals[8], totals[9], totals[10], totals[11], totals[12], totals[13], totals[14], totals[15], totals[16])
```

```python
import functools

import jax
import jax.numpy as jnp
from jax import lax
from jax.experimental import pallas as pl
from jax.experimental.pallas import tpu as pltpu
from jax.sharding import PartitionSpec as P

HD = 128
TOP = 4
LANES = 128

EPS = 1e-06
ROPE_BASE = 1000000.0
NEGATIVE = -1e30
F32 = jnp.float32
BF16 = jnp.bfloat16


def up_to(value, multiple):
    return -(-value // multiple) * multiple


def rotary_tables(positions, head_size):
    half_size = head_size // 2
    exponent = 2.0 * jnp.arange(half_size, dtype=F32) / head_size
    inverse = ROPE_BASE ** (-exponent)
    angles = positions.astype(F32)[:, None] * inverse[None, :]
    cosine_half = jnp.cos(angles)
    sine_half = jnp.sin(angles)
    return (
        jnp.concatenate([cosine_half, cosine_half], axis=1),
        jnp.concatenate([sine_half, sine_half], axis=1),
    )


def rotate(values, cosine_table, sine_table):
    half_size = values.shape[-1] // 2
    first_half = values[..., :half_size]
    second_half = values[..., half_size:]
    turned = jnp.concatenate([-second_half, first_half], axis=-1)
    return values * cosine_table + turned * sine_table


def swap(value, axis, bit):
    size = lax.axis_size(axis)
    return lax.ppermute(value, axis, [(i, i ^ bit) for i in range(size)])


def shift(value, axis, by):
    size = lax.axis_size(axis)
    return lax.ppermute(value, axis, [(i, (i + by) % size) for i in range(size)])


def spread(value, axis):
    size = lax.axis_size(axis)
    held = {0: value}
    bit = size // 2
    while bit:
        held.update({s ^ bit: swap(v, axis, bit) for s, v in list(held.items())})
        bit //= 2
    return [held[s] for s in range(size)]


def collect(parts, axis):
    held = dict(enumerate(parts))
    bit = 1
    while bit < len(parts):
        sent = {s: swap(v, axis, bit) for s, v in held.items() if s & bit}
        held = {
            s: (v.astype(F32) + sent[s ^ bit].astype(F32)).astype(v.dtype)
            for s, v in held.items()
            if not s & bit
        }
        bit *= 2
    return held[0]


def rows_at(value, start, size):
    return lax.dynamic_slice_in_dim(value, start, size, axis=0)


def in_order(pieces, index, axis):
    size = pieces[0].shape[axis]
    shape = list(pieces[0].shape)
    shape[axis] = size * len(pieces)
    whole = jnp.zeros(shape, pieces[0].dtype)
    for piece, place in zip(pieces, index):
        whole = lax.dynamic_update_slice_in_dim(whole, piece, place * size, axis)
    return whole


def gather_over_tensor(piece):
    size = lax.axis_size("tensor")
    me = lax.axis_index("tensor")
    pieces = [piece] + [shift(piece, "tensor", k) for k in range(1, size)]
    return in_order(pieces, [(me - k) % size for k in range(size)], 0)


def dot_tt(a, b):
    return lax.dot_general(a, b, (((1,), (1,)), ((), ())), preferred_element_type=F32)


def dot_nt(a, b):
    return lax.dot_general(a, b, (((0,), (0,)), ((), ())), preferred_element_type=F32)


def dot(a, b):
    return jnp.dot(a, b, preferred_element_type=F32)


def attend_kernel(place_ref, q_ref, *refs, groups, score_scale):
    kv_refs = refs[:groups]
    out_ref, log_ref, peak, total, mix = refs[groups:]
    me, length = place_ref[0], place_ref[1]
    rows = q_ref.shape[0]
    query = q_ref[...]

    def block(s):
        key, value = kv_refs[s][:, :HD], kv_refs[s][:, HD:]
        scores = dot_tt(query, key) * score_scale
        column = lax.broadcasted_iota(jnp.int32, (rows, rows), 1)
        good = column < length - (me ^ s) * rows
        if s == 0:
            good &= column <= lax.broadcasted_iota(jnp.int32, (rows, rows), 0)
        scores = jnp.where(good, scores, NEGATIVE)
        here = jnp.max(scores, axis=1, keepdims=True)
        if s == 0:
            lifted = jnp.exp(scores - here)
            peak[...] = here
            total[...] = jnp.sum(lifted, axis=1, keepdims=True)
            mix[...] = dot(lifted.astype(BF16), value)
        else:
            new_peak = jnp.maximum(peak[...], here)
            keep = jnp.exp(peak[...] - new_peak)
            lifted = jnp.exp(scores - new_peak)
            peak[...] = new_peak
            total[...] = total[...] * keep + jnp.sum(lifted, axis=1, keepdims=True)
            mix[...] = mix[...] * keep + dot(lifted.astype(BF16), value)

    block(0)
    for s in range(1, groups):
        pl.when(((me ^ s) < me) & ((me ^ s) * rows < length))(functools.partial(block, s))
    out_ref[...] = (mix[...] / total[...]).astype(BF16)
    log_ref[0] = peak[...] + jnp.log(total[...])


def attend(place, query, kv, heads, score_scale):
    rows = query.shape[0]
    groups = len(kv)
    spec = pltpu.PrefetchScalarGridSpec(
        num_scalar_prefetch=1,
        grid=(heads,),
        in_specs=[pl.BlockSpec((rows, HD), lambda h, p: (0, h))]
        + [pl.BlockSpec((rows, 2 * HD), lambda h, p: (0, h))] * groups,
        out_specs=[
            pl.BlockSpec((rows, HD), lambda h, p: (0, h)),
            pl.BlockSpec((1, rows, 1), lambda h, p: (h, 0, 0)),
        ],
        scratch_shapes=[
            pltpu.VMEM((rows, 1), F32),
            pltpu.VMEM((rows, 1), F32),
            pltpu.VMEM((rows, HD), F32),
        ],
    )
    work = heads * rows * rows * groups
    return pl.pallas_call(
        functools.partial(attend_kernel, groups=groups, score_scale=score_scale),
        grid_spec=spec,
        out_shape=[
            jax.ShapeDtypeStruct((rows, heads * HD), BF16),
            jax.ShapeDtypeStruct((heads, rows, 1), F32),
        ],
        compiler_params=pltpu.CompilerParams(vmem_limit_bytes=40 << 20),
        cost_estimate=pl.CostEstimate(
            flops=4 * work * HD, bytes_accessed=6 << 20, transcendentals=work
        ),
    )(place, query, *kv)


def attend_back_kernel(place_ref, q_ref, g_ref, o_ref, log_ref, *refs, groups, score_scale):
    kv_refs = refs[:groups]
    dq_ref = refs[groups]
    dkv_refs = refs[groups + 1 : 2 * groups + 1]
    total = refs[2 * groups + 1]
    me, length = place_ref[0], place_ref[1]
    rows = q_ref.shape[0]
    query, grad = q_ref[...], g_ref[...]
    log_sum = log_ref[0]
    centre = jnp.sum(grad.astype(F32) * o_ref[...].astype(F32), axis=1, keepdims=True)

    def block(s):
        key, value = kv_refs[s][:, :HD], kv_refs[s][:, HD:]
        scores = dot_tt(query, key) * score_scale
        column = lax.broadcasted_iota(jnp.int32, (rows, rows), 1)
        good = column < length - (me ^ s) * rows
        if s == 0:
            good &= column <= lax.broadcasted_iota(jnp.int32, (rows, rows), 0)
        weights = jnp.exp(jnp.where(good, scores, NEGATIVE) - log_sum)
        weight_grad = dot_tt(grad, value)
        score_grad = (weights * (weight_grad - centre)).astype(BF16)
        query_grad = dot(score_grad, key)
        if s == 0:
            total[...] = query_grad
        else:
            total[...] += query_grad
        dkv_refs[s][:, :HD] = (dot_nt(score_grad, query) * score_scale).astype(BF16)
        dkv_refs[s][:, HD:] = dot_nt(weights.astype(BF16), grad).astype(BF16)

    def nothing(s):
        dkv_refs[s][...] = jnp.zeros_like(dkv_refs[s])

    block(0)
    for s in range(1, groups):
        seen = ((me ^ s) < me) & ((me ^ s) * rows < length)
        pl.when(seen)(functools.partial(block, s))
        pl.when(jnp.logical_not(seen))(functools.partial(nothing, s))
    dq_ref[...] = total[...] * score_scale


def attend_back(place, query, grad, out, log_sums, kv, heads, score_scale):
    rows = query.shape[0]
    groups = len(kv)
    head = pl.BlockSpec((rows, HD), lambda h, p: (0, h))
    pair = pl.BlockSpec((rows, 2 * HD), lambda h, p: (0, h))
    spec = pltpu.PrefetchScalarGridSpec(
        num_scalar_prefetch=1,
        grid=(heads,),
        in_specs=[head, head, head, pl.BlockSpec((1, rows, 1), lambda h, p: (h, 0, 0))]
        + [pair] * groups,
        out_specs=[head] + [pair] * groups,
        scratch_shapes=[pltpu.VMEM((rows, HD), F32)],
    )
    work = heads * rows * rows * groups
    return pl.pallas_call(
        functools.partial(attend_back_kernel, groups=groups, score_scale=score_scale),
        grid_spec=spec,
        out_shape=[jax.ShapeDtypeStruct((rows, heads * HD), F32)]
        + [jax.ShapeDtypeStruct((rows, 2 * heads * HD), BF16)] * groups,
        compiler_params=pltpu.CompilerParams(vmem_limit_bytes=48 << 20),
        cost_estimate=pl.CostEstimate(
            flops=10 * work * HD, bytes_accessed=12 << 20, transcendentals=work
        ),
    )(place, query, grad, out, log_sums, *kv)


def mixture_kernel(
    mix_ref, hidden_grad_ref, kept_ref, spot_ref, router_ref, weight_ref,
    lin_grad_ref, hidden_ref, small_ref, part_ref,
    total, probs_ref, logits_ref, gate_grad_ref, *, experts, local,
):
    step = pl.program_id(0)
    width = hidden_ref.shape[1]
    mix = mix_ref[...]
    lane = lax.broadcasted_iota(jnp.int32, kept_ref.shape, 1)

    @pl.when(step == 0)
    def _():
        logits = dot(mix, router_ref[...])
        logits_ref[...] = logits
        masked = jnp.where(lane < experts, logits, NEGATIVE)
        lifted = jnp.exp(masked - jnp.max(masked, axis=1, keepdims=True))
        probs_ref[...] = lifted / jnp.sum(lifted, axis=1, keepdims=True)
        gate_grad_ref[...] = jnp.zeros_like(gate_grad_ref)
        total[...] = jnp.zeros_like(total)

    spot = spot_ref[pl.ds(step, 1), :]
    kept = kept_ref[...].astype(F32)
    gate = jnp.sum(probs_ref[...] * kept * spot, axis=1, keepdims=True)
    switch = jax.nn.sigmoid(jnp.sum(logits_ref[...] * spot, axis=1, keepdims=True))
    routed = step < local
    scale = jnp.where(routed, gate, switch)
    weight = weight_ref[...]
    lin = dot(mix, weight)
    gate_lin, up_lin = lin[:, :width], lin[:, width:]
    logistic = jax.nn.sigmoid(gate_lin)
    silu = gate_lin * logistic
    hidden = silu * up_lin
    hidden_grad = hidden_grad_ref[...]
    row_sum = jnp.sum(hidden * hidden_grad, axis=1, keepdims=True)
    factor = jnp.where(routed, jnp.sum(kept * spot, axis=1, keepdims=True), switch * (1.0 - switch))
    gate_grad_ref[...] += row_sum * factor * spot
    hidden_ref[...] = (scale * hidden).astype(BF16)
    scaled = scale * hidden_grad
    lin_grad_ref[:, :width] = (
        scaled * up_lin * logistic * (1.0 + gate_lin * (1.0 - logistic))
    ).astype(BF16)
    lin_grad_ref[:, width:] = (scaled * silu).astype(BF16)
    total[...] += dot_tt(lin_grad_ref[...], weight)

    @pl.when(step == local)
    def _():
        grads = gate_grad_ref[...]
        probs = probs_ref[...]
        routed_grads = jnp.where(lane < experts, grads, 0.0)
        inner = jnp.sum(probs * routed_grads, axis=1, keepdims=True)
        small = jnp.where(lane < experts, probs * (grads - inner), grads).astype(BF16)
        small_ref[...] = small
        part_ref[...] = (total[...] + dot_tt(small, router_ref[...])).astype(BF16)


def mixture_chunk(mix, hidden_grad, kept, spot, router, weight, experts, local):
    rows, depth = mix.shape
    steps = local + 1
    pair = weight.shape[1] // steps
    width = pair // 2
    whole = lambda shape: pl.BlockSpec(shape, lambda j: (0, 0))
    return pl.pallas_call(
        functools.partial(mixture_kernel, experts=experts, local=local),
        grid=(steps,),
        in_specs=[
            whole((rows, depth)),
            pl.BlockSpec((rows, width), lambda j: (0, j)),
            whole((rows, LANES)),
            whole(spot.shape),
            whole((depth, LANES)),
            pl.BlockSpec((depth, pair), lambda j: (0, j)),
        ],
        out_specs=[
            pl.BlockSpec((rows, pair), lambda j: (0, j)),
            pl.BlockSpec((rows, width), lambda j: (0, j)),
            whole((rows, LANES)),
            whole((rows, depth)),
        ],
        out_shape=[
            jax.ShapeDtypeStruct((rows, steps * pair), BF16),
            jax.ShapeDtypeStruct((rows, steps * width), BF16),
            jax.ShapeDtypeStruct((rows, LANES), BF16),
            jax.ShapeDtypeStruct((rows, depth), BF16),
        ],
        scratch_shapes=[
            pltpu.VMEM((rows, depth), F32),
            pltpu.VMEM((rows, LANES), F32),
            pltpu.VMEM((rows, LANES), F32),
            pltpu.VMEM((rows, LANES), F32),
        ],
        compiler_params=pltpu.CompilerParams(vmem_limit_bytes=56 << 20),
        cost_estimate=pl.CostEstimate(
            flops=4 * rows * depth * steps * pair,
            bytes_accessed=20 << 20,
            transcendentals=rows * steps * width,
        ),
    )(mix, hidden_grad, kept, spot, router, weight)


def shards(
    layer_input,
    attention_gain,
    query_weight,
    key_weight,
    value_weight,
    query_bias,
    key_bias,
    value_bias,
    output_weight,
    mixture_gain,
    router_weight,
    expert_gate,
    expert_up,
    expert_down,
    shared_gate,
    shared_up,
    shared_down,
    shared_switch,
    slot_lengths,
    routes,
    cotangent,
):
    rows, depth = layer_input.shape[1:]
    groups = lax.axis_size("expert")
    tensors = lax.axis_size("tensor")
    slots = lax.axis_size("dp")
    slot_at = lax.axis_index("dp")
    block_at = lax.axis_index("expert")
    tensor_at = lax.axis_index("tensor")
    experts = router_weight.shape[1]
    local, _, expert_units = expert_gate.shape
    shared_units = shared_gate.shape[1] // groups
    capacity = rows * TOP // experts
    score_scale = HD ** (-0.5)
    heads_here = query_weight.shape[1] // HD
    wide = heads_here * HD
    piece = rows // tensors
    width = up_to(max(expert_units, shared_units), LANES)
    pair = 2 * width
    steps = local + 1
    length = slot_lengths[0]
    positions = block_at * rows + jnp.arange(rows, dtype=jnp.int32)
    live_rows = positions < length
    place = jnp.stack([block_at.astype(jnp.int32), length])

    qkv_full = lax.all_gather(
        jnp.concatenate([query_weight, key_weight, value_weight], axis=1),
        ("dp", "expert"), axis=0, tiled=True,
    )
    output_wide = [output_weight] + [shift(output_weight, "tensor", k) for k in range(1, tensors)]
    output_wide = in_order(output_wide, [(tensor_at - k) % tensors for k in range(tensors)], 1)
    output_full = lax.all_gather(output_wide, ("dp", "expert"), axis=0, tiled=True)

    route_block = routes[0]
    expert_ids = jnp.arange(experts, dtype=jnp.int32)
    chosen = jnp.any(route_block[:, :, None] == expert_ids[None, None, :], axis=1) & live_rows[:, None]
    row_ids = jnp.arange(rows, dtype=jnp.int32)
    earlier = (row_ids[None, :] < row_ids[:, None]).astype(BF16)
    before = dot(earlier, chosen.astype(BF16))
    kept = chosen & (before < capacity)
    kept = jnp.pad(kept.astype(BF16), ((0, 0), (0, LANES - experts)))
    kept_blocks = spread(kept, "expert")

    shared_own = jnp.stack([shared_gate, shared_up, shared_down])
    own_rows = shared_own.shape[1]

    def units_of(block):
        return lax.dynamic_slice_in_dim(shared_own, block * shared_units, shared_units, axis=2)

    shared_pieces = [units_of(block_at)] + [
        swap(units_of(block_at ^ s), "expert", s) for s in range(1, groups)
    ]
    shared_half = in_order(shared_pieces, [block_at ^ s for s in range(groups)], 1)
    halves = [shared_half] + [shift(shared_half, "dp", k) for k in range(1, slots)]
    shared_all = in_order(halves, [(slot_at - k) % slots for k in range(slots)], 1)

    def pad_units(weight):
        return jnp.pad(weight, ((0, 0), (0, width - weight.shape[1])))

    weight_parts = []
    for j in range(local):
        weight_parts += [pad_units(expert_gate[j]), pad_units(expert_up[j])]
    weight_parts += [pad_units(shared_all[0]), pad_units(shared_all[1])]
    lin_weight = jnp.concatenate(weight_parts, axis=1)
    down_weight = jnp.concatenate(
        [pad_units(expert_down[j]) for j in range(local)] + [pad_units(shared_all[2])], axis=1
    )
    small_weight = jnp.pad(
        jnp.concatenate([router_weight, shared_switch[:, None]], axis=1),
        ((0, 0), (0, LANES - experts - 1)),
    )
    spot_at = jnp.concatenate(
        [block_at * local + jnp.arange(local, dtype=jnp.int32), jnp.full((1,), experts, jnp.int32)]
    )
    spot = (spot_at[:, None] == jnp.arange(LANES, dtype=jnp.int32)[None, :]).astype(F32)
    spot = jnp.pad(spot, ((0, up_to(steps, 8) - steps), (0, 0)))

    inputs = layer_input[0].astype(F32)
    gain_one = attention_gain.astype(F32)
    inverse_one = lax.rsqrt(jnp.mean(inputs * inputs, axis=1, keepdims=True) + EPS)
    normed = (inputs * inverse_one * gain_one).astype(BF16)
    bias = jnp.concatenate([query_bias, key_bias, value_bias]).astype(F32)
    pre = dot(normed, qkv_full) + bias
    cosine_table, sine_table = rotary_tables(positions, HD)
    cosine_table = cosine_table[:, None, :]
    sine_table = sine_table[:, None, :]
    pre = pre.reshape(rows, 3, heads_here, HD)
    queries = rotate(pre[:, 0], cosine_table, sine_table).astype(BF16).reshape(rows, wide)
    keys = rotate(pre[:, 1], cosine_table, sine_table).astype(BF16)
    values = pre[:, 2].astype(BF16)
    kv = spread(jnp.stack([keys, values], axis=2).reshape(rows, 2 * wide), "expert")
    heads_low, log_sums = attend(place, queries, kv, heads_here, score_scale)

    def rows_of(value, index):
        return rows_at(value, index * piece, piece)

    mine = [rows_of(heads_low, tensor_at)] + [
        shift(rows_of(heads_low, (tensor_at + k) % tensors), "tensor", k) for k in range(1, tensors)
    ]
    heads_rows = in_order(mine, [(tensor_at - k) % tensors for k in range(tensors)], 1)
    attended = dot_tt(heads_rows, output_full)
    inputs_own = rows_of(inputs, tensor_at)
    live_own = rows_of(live_rows, tensor_at)[:, None]
    residual = inputs_own + attended
    gain_two = mixture_gain.astype(F32)
    inverse_two = lax.rsqrt(jnp.mean(residual * residual, axis=1, keepdims=True) + EPS)
    mix_own = (residual * inverse_two * gain_two).astype(BF16)

    upstream_low = jnp.where(live_rows[:, None], cotangent[0], jnp.zeros((), BF16))
    upstream_blocks = spread(upstream_low, "expert")

    lin_grads, hiddens, smalls, mixes, ups, sums = [], [], [], [], [], []
    for k in range(tensors):
        at = (tensor_at + k) % tensors
        arrived = mix_own if k == 0 else shift(mix_own, "tensor", tensors - k)
        mix = jnp.concatenate(spread(arrived, "expert"), axis=0)
        up = jnp.concatenate([rows_of(u, at) for u in upstream_blocks], axis=0)
        kept_here = jnp.concatenate([rows_of(m, at) for m in kept_blocks], axis=0)
        hidden_grad = dot(up, down_weight)
        lin_grad, hidden, small, part = mixture_chunk(
            mix, hidden_grad, kept_here, spot, small_weight, lin_weight, experts, local
        )
        parts = [part[s * piece : (s + 1) * piece] for s in range(groups)]
        total = collect(parts, "expert")
        sums.append(total if k == 0 else shift(total, "tensor", k))
        lin_grads.append(lin_grad)
        hiddens.append(hidden)
        smalls.append(small)
        mixes.append(mix)
        ups.append(up)

    mix_grad = sum(s.astype(F32) for s in sums)
    scaled_two = mix_grad * gain_two
    mixture_gain_grad = jnp.sum(mix_grad * residual * inverse_two, axis=0)
    upstream_own = rows_of(upstream_low, tensor_at).astype(F32)
    residual_grad = (
        upstream_own
        + inverse_two * scaled_two
        - residual * inverse_two**3 * jnp.mean(scaled_two * residual, axis=1, keepdims=True)
    )
    attended_grad = residual_grad.astype(BF16)
    heads_grad_rows = dot(attended_grad, output_full).astype(BF16)

    def heads_of(index):
        return lax.dynamic_slice_in_dim(heads_grad_rows, index * wide, wide, axis=1)

    grads_in = [heads_of(tensor_at)] + [
        shift(heads_of((tensor_at + k) % tensors), "tensor", k) for k in range(1, tensors)
    ]
    heads_grad = in_order(grads_in, [(tensor_at - k) % tensors for k in range(tensors)], 0)
    query_grads, *kv_grads = attend_back(
        place, queries, heads_grad, heads_low, log_sums, kv, heads_here, score_scale
    )
    kv_sum = collect(kv_grads, "expert").astype(F32).reshape(rows, heads_here, 2, HD)
    query_pre_grad = rotate(query_grads.reshape(rows, heads_here, HD), cosine_table, -sine_table)
    key_pre_grad = rotate(kv_sum[:, :, 0], cosine_table, -sine_table)
    pre_grad = jnp.concatenate(
        [
            query_pre_grad.astype(BF16).reshape(rows, wide),
            key_pre_grad.astype(BF16).reshape(rows, wide),
            kv_sum[:, :, 1].astype(BF16).reshape(rows, wide),
        ],
        axis=1,
    )
    normed_part = dot_tt(pre_grad, qkv_full).astype(BF16)
    normed_rows = [rows_of(normed_part, tensor_at)] + [
        shift(rows_of(normed_part, (tensor_at + k) % tensors), "tensor", k)
        for k in range(1, tensors)
    ]
    normed_grad = sum(n.astype(F32) for n in normed_rows)
    inverse_own = rows_of(inverse_one, tensor_at)
    scaled_one = normed_grad * gain_one
    attention_gain_grad = jnp.sum(normed_grad * inputs_own * inverse_own, axis=0)
    input_grad = (
        residual_grad
        + inverse_own * scaled_one
        - inputs_own * inverse_own**3 * jnp.mean(scaled_one * inputs_own, axis=1, keepdims=True)
    )
    input_grad = gather_over_tensor(input_grad.astype(BF16)).astype(F32)

    lin_all = jnp.concatenate(lin_grads, axis=0)
    hidden_all = jnp.concatenate(hiddens, axis=0)
    small_all = jnp.concatenate(smalls, axis=0)
    mix_all = jnp.concatenate(mixes, axis=0)
    up_all = jnp.concatenate(ups, axis=0)
    down_grad = dot_nt(hidden_all, up_all).astype(BF16)
    lin_weight_grad = dot_nt(lin_all, mix_all).astype(BF16)
    small_grad = dot_nt(mix_all, small_all)[:, : experts + 1]

    def total_over_slots(part):
        whole = part.astype(F32)
        for k in range(1, slots):
            whole += shift(part, "dp", k).astype(F32)
        return whole

    expert_grads = [[], [], []]
    for j in range(local):
        first = j * pair
        found = (
            lin_weight_grad[first : first + expert_units],
            lin_weight_grad[first + width : first + width + expert_units],
            down_grad[j * width : j * width + expert_units],
        )
        for store, part in zip(expert_grads, found):
            store.append(total_over_slots(part).T)
    expert_grads = [jnp.stack(store) for store in expert_grads]

    first = local * pair
    shared_part = jnp.stack(
        [
            lin_weight_grad[first : first + shared_units],
            lin_weight_grad[first + width : first + width + shared_units],
            down_grad[local * width : local * width + shared_units],
        ]
    )
    half = depth // slots

    def half_of(index):
        return lax.dynamic_slice_in_dim(shared_part, index * half, half, axis=2)

    shared_sum = half_of(slot_at).astype(F32)
    for k in range(1, slots):
        shared_sum += shift(half_of((slot_at + k) % slots), "dp", k).astype(F32)
    shared_sum = shared_sum.astype(BF16)

    def owned_by(block):
        return lax.dynamic_slice_in_dim(shared_sum, block * own_rows, own_rows, axis=2)

    shared_back = [owned_by(block_at)] + [
        swap(owned_by(block_at ^ s), "expert", s) for s in range(1, groups)
    ]
    shared_grads = in_order(shared_back, [block_at ^ s for s in range(groups)], 1)
    shared_grads = shared_grads.astype(F32).transpose(0, 2, 1)

    attended_all = lax.all_gather(attended_grad, "tensor", axis=0, tiled=True)
    output_grad = lax.psum_scatter(
        dot_nt(attended_all, heads_low).astype(BF16), ("dp", "expert"), scatter_dimension=0, tiled=True
    ).astype(F32)
    qkv_grad = lax.psum_scatter(
        dot_nt(normed, pre_grad).astype(BF16), ("dp", "expert"), scatter_dimension=0, tiled=True
    ).astype(F32)

    mixture_sums = []
    for k in range(tensors):
        part = dot_tt(hiddens[k], down_weight).astype(BF16)
        parts = [part[s * piece : (s + 1) * piece] for s in range(groups)]
        total = collect(parts, "expert")
        mixture_sums.append(total if k == 0 else shift(total, "tensor", k))
    mixture = sum(s.astype(F32) for s in mixture_sums)
    output_own = jnp.where(live_own, residual + mixture, 0.0).astype(BF16)
    layer_output = gather_over_tensor(output_own)

    bias_grad = jnp.sum(pre_grad.astype(F32), axis=0)
    bias_place = lax.dynamic_update_slice_in_dim(
        jnp.zeros((tensors * 3 * wide,), F32), bias_grad, tensor_at * 3 * wide, axis=0
    )
    packed = jnp.concatenate(
        [attention_gain_grad, mixture_gain_grad, small_grad.T.reshape(-1), bias_place]
    )
    packed = lax.psum(packed, ("dp", "expert", "tensor"))
    small_total = packed[2 * depth : (3 + experts) * depth].reshape(experts + 1, depth)
    bias_total = lax.dynamic_slice_in_dim(
        packed, (3 + experts) * depth + tensor_at * 3 * wide, 3 * wide, axis=0
    )
    return (
        layer_output[None],
        input_grad[None],
        packed[:depth],
        qkv_grad[:, :wide],
        qkv_grad[:, wide : 2 * wide],
        qkv_grad[:, 2 * wide :],
        bias_total[:wide],
        bias_total[wide : 2 * wide],
        bias_total[2 * wide :],
        output_grad,
        packed[depth : 2 * depth],
        small_total[:experts].T,
        expert_grads[0],
        expert_grads[1],
        expert_grads[2],
        shared_grads[0],
        shared_grads[1],
        shared_grads[2],
        small_total[experts],
    )


def solution(mesh):
    dense = P(("dp", "expert"), "tensor")
    routed = P("expert", None, "tensor")
    rows = P("dp", "expert", None)
    in_specs = (
        rows, P(), dense, dense, dense, P("tensor"), P("tensor"), P("tensor"), dense, P(), P(),
        routed, routed, routed, dense, dense, dense, P(), P("dp"), rows, rows,
    )
    out_specs = (
        rows, rows, P(), dense, dense, dense, P("tensor"), P("tensor"), P("tensor"), dense, P(), P(),
        routed, routed, routed, dense, dense, dense, P(),
    )
    return jax.shard_map(shards, mesh=mesh, in_specs=in_specs, out_specs=out_specs, check_vma=False)
```

```python
import functools

import jax
import jax.numpy as jnp
from jax import lax
from jax.experimental import pallas as pl
from jax.experimental.pallas import tpu as pltpu
from jax.sharding import PartitionSpec as P

HD = 128
TOP = 4
LANES = 128

EPS = 1e-06
ROPE_BASE = 1000000.0
NEGATIVE = -1e30
F32 = jnp.float32
QUICK = pl.CostEstimate(flops=0, bytes_accessed=1 << 20, transcendentals=0)
BF16 = jnp.bfloat16


def up_to(value, multiple):
    return -(-value // multiple) * multiple


def rotary_tables(positions, head_size):
    half_size = head_size // 2
    exponent = 2.0 * jnp.arange(half_size, dtype=F32) / head_size
    inverse = ROPE_BASE ** (-exponent)
    angles = positions.astype(F32)[:, None] * inverse[None, :]
    cosine_half = jnp.cos(angles)
    sine_half = jnp.sin(angles)
    return (
        jnp.concatenate([cosine_half, cosine_half], axis=1),
        jnp.concatenate([-sine_half, sine_half], axis=1),
    )


class Links:
    def __init__(self):
        self.last = {}

    def send(self, link, values, axis, perms):
        before = None if link == "core" else self.last.get(link)
        if before is not None:
            tied = lax.optimization_barrier((tuple(values), before))
            values = tied[0]
        with jax.named_scope("over_" + link):
            arrived = tuple(lax.ppermute(v, axis, p) for v, p in zip(values, perms))
        self.last[link] = arrived
        return list(arrived)

    def swap(self, value, axis, bit):
        link = "x" if axis == "dp" else "core" if bit == 1 else "y"
        size = lax.axis_size(axis)
        return self.send(link, [value], axis, [[(i, i ^ bit) for i in range(size)]])[0]

    def swaps(self, values, axis):
        size = lax.axis_size(axis)
        perms = [[(i, i ^ s) for i in range(size)] for s in range(1, size)]
        return self.send("y", values, axis, perms)

    def shift(self, value, axis, by):
        size = lax.axis_size(axis)
        perm = [(i, (i + by) % size) for i in range(size)]
        return self.send("x" if axis == "dp" else "z", [value], axis, [perm])[0]

    def shifts(self, values, axis, direction=1):
        link = "x" if axis == "dp" else "z"
        size = lax.axis_size(axis)
        perms = [[(i, (i + direction * k) % size) for i in range(size)] for k in range(1, size)]
        return self.send(link, values, axis, perms[: len(values)])

    def spread(self, value, axis, low=1):
        bit = lax.axis_size(axis) // 2
        while bit >= low:
            value = jnp.concatenate([value, self.swap(value, axis, bit)], axis=0)
            bit //= 2
        return value

    def meet(self, near, far, axis, bit):
        arrived = self.swap(far, axis, bit)
        return (near.astype(F32) + arrived.astype(F32)).astype(near.dtype)

    def scatter(self, value, axis, wait):
        at = lax.axis_index(axis)
        bit = 1
        while value.shape[0] > 1:
            value = value.reshape(value.shape[0] // 2, 2, *value.shape[1:])
            own = lax.rem(at // bit, 2)
            near, far = (
                lax.dynamic_index_in_dim(value, i, axis=1, keepdims=False) for i in (own, 1 - own)
            )
            value = self.meet(near, far, axis, bit)
            if bit == 1:
                value = after(value, wait)
            bit *= 2
        return value[0]

    def collect(self, near, far, axis, low=1):
        bit = low
        while True:
            arrived = self.swap(far, axis, bit)
            near = (near.astype(F32) + arrived.astype(F32)).astype(near.dtype)
            bit *= 2
            if bit >= lax.axis_size(axis):
                return near
            half = near.shape[0] // 2
            near, far = near[:half], near[half:]


def sum_over_all(value, axes):
    for axis in axes:
        size = lax.axis_size(axis)
        bit = 1
        while bit < size:
            value = value + lax.ppermute(value, axis, [(i, i ^ bit) for i in range(size)])
            bit *= 2
    return value


def reversed_order(size):
    order, bit = [0], size // 2
    while bit:
        order = order + [i ^ bit for i in order]
        bit //= 2
    return order


def after(value, *others):
    return lax.optimization_barrier((value, others))[0]


def together(*values):
    return lax.optimization_barrier(values)


def rows_at(value, start, size):
    return lax.dynamic_slice_in_dim(value, start, size, axis=0)


def in_order(pieces, index, axis):
    size = pieces[0].shape[axis]
    shape = list(pieces[0].shape)
    shape[axis] = size * len(pieces)
    whole = jnp.zeros(shape, pieces[0].dtype)
    for piece, place in zip(pieces, index):
        whole = lax.dynamic_update_slice_in_dim(whole, piece, place * size, axis)
    return whole


def dot_tt(a, b):
    return lax.dot_general(a, b, (((1,), (1,)), ((), ())), preferred_element_type=F32)


def dot_nt(a, b):
    return lax.dot_general(a, b, (((0,), (0,)), ((), ())), preferred_element_type=F32)


def dot(a, b):
    return jnp.dot(a, b, preferred_element_type=F32)


def project_kernel(
    rows_ref, wq_ref, wk_ref, wv_ref, bq_ref, bk_ref, bv_ref, cosine_ref, sine_ref, q_ref, kv_ref
):
    source = rows_ref[...]
    cosine, sine = cosine_ref[...], sine_ref[...]

    def turned(value):
        return value * cosine + pltpu.roll(value, HD // 2, 1) * sine

    query = dot(source, wq_ref[...]) + bq_ref[...].astype(F32)
    key = dot(source, wk_ref[...]) + bk_ref[...].astype(F32)
    value = dot(source, wv_ref[...]) + bv_ref[...].astype(F32)
    for i in range(q_ref.shape[1] // HD):
        here = slice(i * HD, (i + 1) * HD)
        q_ref[:, here] = turned(query[:, here]).astype(BF16)
        kv_ref[:, 2 * i * HD : (2 * i + 1) * HD] = turned(key[:, here]).astype(BF16)
        kv_ref[:, (2 * i + 1) * HD : (2 * i + 2) * HD] = value[:, here].astype(BF16)


def project(source, weight, bias, cosine, sine):
    rows, depth = source.shape
    wide = weight.shape[1] // 3
    block = 2 * HD
    steps = wide // block
    whole = lambda shape: pl.BlockSpec(shape, lambda h: (0, 0))
    third = lambda size, i: pl.BlockSpec((size, block), lambda h: (0, i * steps + h))
    return pl.pallas_call(
        project_kernel,
        grid=(steps,),
        in_specs=[whole((rows, depth))]
        + [third(depth, i) for i in range(3)]
        + [third(1, i) for i in range(3)]
        + [whole((rows, HD))] * 2,
        out_specs=[
            pl.BlockSpec((rows, block), lambda h: (0, h)),
            pl.BlockSpec((rows, 2 * block), lambda h: (0, h)),
        ],
        out_shape=[
            jax.ShapeDtypeStruct((rows, wide), BF16),
            jax.ShapeDtypeStruct((rows, 2 * wide), BF16),
        ],
        compiler_params=pltpu.CompilerParams(vmem_limit_bytes=40 << 20),
        cost_estimate=QUICK,
    )(source, weight, weight, weight, bias, bias, bias, cosine, sine)


def turn_back_kernel(dq_ref, dkv_ref, cosine_ref, sine_ref, out_ref, sum_ref):
    cosine, sine = cosine_ref[...], sine_ref[...]
    wide = dq_ref.shape[1]

    def turned(value):
        return value * cosine - pltpu.roll(value, HD // 2, 1) * sine

    def store(at, value):
        low = value.astype(BF16)
        out_ref[:, at : at + HD] = low
        sum_ref[:, at : at + HD] = jnp.sum(low.astype(F32), axis=0, keepdims=True)

    for i in range(wide // HD):
        at = i * HD
        store(at, turned(dq_ref[:, at : at + HD]))
        here, there = slice(2 * at, 2 * at + HD), slice(2 * at + HD, 2 * at + 2 * HD)
        store(wide + at, turned(dkv_ref[:, here].astype(F32)))
        store(2 * wide + at, dkv_ref[:, there].astype(F32))


def turn_back(query_grads, kv_grads, cosine, sine):
    rows, wide = query_grads.shape
    return pl.pallas_call(
        turn_back_kernel,
        out_shape=[
            jax.ShapeDtypeStruct((rows, 3 * wide), BF16),
            jax.ShapeDtypeStruct((1, 3 * wide), F32),
        ],
        compiler_params=pltpu.CompilerParams(vmem_limit_bytes=40 << 20),
        cost_estimate=QUICK,
    )(query_grads, kv_grads, cosine, sine)


def attend_kernel(place_ref, q_ref, kv_ref, out_ref, log_ref, peak, total, mix, *, groups, score_scale):
    me, length = place_ref[0], place_ref[1]
    rows = q_ref.shape[0]
    query = q_ref[...]
    peak[...] = jnp.full_like(peak, NEGATIVE)
    total[...] = jnp.zeros_like(total)
    mix[...] = jnp.zeros_like(mix)

    def block(j, last):
        here = slice(j * rows, (j + 1) * rows)
        key, value = kv_ref[here, :HD], kv_ref[here, HD:]
        scores = dot_tt(query, key) * score_scale
        column = lax.broadcasted_iota(jnp.int32, (rows, rows), 1)
        good = column < length - j * rows
        if last:
            good &= column <= lax.broadcasted_iota(jnp.int32, (rows, rows), 0)
        scores = jnp.where(good, scores, NEGATIVE)
        new_peak = jnp.maximum(peak[...], jnp.max(scores, axis=1, keepdims=True))
        keep = jnp.exp(peak[...] - new_peak)
        lifted = jnp.exp(scores - new_peak)
        peak[...] = new_peak
        total[...] = total[...] * keep + jnp.sum(lifted, axis=1, keepdims=True)
        mix[...] = mix[...] * keep + dot(lifted.astype(BF16), value)

    for j in range(groups):
        alive = j * rows < length
        pl.when((j < me) & alive)(functools.partial(block, j, False))
        pl.when((j == me) & alive)(functools.partial(block, j, True))
    out_ref[...] = (mix[...] / total[...]).astype(BF16)
    log_ref[0] = peak[...] + jnp.log(total[...])


def attend(place, query, kv, heads, score_scale):
    rows = query.shape[0]
    groups = kv.shape[0] // rows
    spec = pltpu.PrefetchScalarGridSpec(
        num_scalar_prefetch=1,
        grid=(heads,),
        in_specs=[
            pl.BlockSpec((rows, HD), lambda h, p: (0, h)),
            pl.BlockSpec((groups * rows, 2 * HD), lambda h, p: (0, h)),
        ],
        out_specs=[
            pl.BlockSpec((rows, HD), lambda h, p: (0, h)),
            pl.BlockSpec((1, rows, 1), lambda h, p: (h, 0, 0)),
        ],
        scratch_shapes=[
            pltpu.VMEM((rows, 1), F32),
            pltpu.VMEM((rows, 1), F32),
            pltpu.VMEM((rows, HD), F32),
        ],
    )
    work = heads * rows * rows * groups
    return pl.pallas_call(
        functools.partial(attend_kernel, groups=groups, score_scale=score_scale),
        grid_spec=spec,
        out_shape=[
            jax.ShapeDtypeStruct((rows, heads * HD), BF16),
            jax.ShapeDtypeStruct((heads, rows, 1), F32),
        ],
        compiler_params=pltpu.CompilerParams(vmem_limit_bytes=40 << 20),
        cost_estimate=QUICK,
    )(place, query, kv)


def attend_back_kernel(
    place_ref, q_ref, g_ref, o_ref, log_ref, kv_ref, dq_ref, dkv_ref, total, *, groups, score_scale
):
    me, length = place_ref[0], place_ref[1]
    rows = q_ref.shape[0]
    query, grad = q_ref[...], g_ref[...]
    log_sum = log_ref[0]
    centre = jnp.sum(grad.astype(F32) * o_ref[...].astype(F32), axis=1, keepdims=True)
    total[...] = jnp.zeros_like(total)

    def block(j, last):
        here = slice(j * rows, (j + 1) * rows)
        key, value = kv_ref[here, :HD], kv_ref[here, HD:]
        scores = dot_tt(query, key) * score_scale
        column = lax.broadcasted_iota(jnp.int32, (rows, rows), 1)
        good = column < length - j * rows
        if last:
            good &= column <= lax.broadcasted_iota(jnp.int32, (rows, rows), 0)
        weights = jnp.exp(jnp.where(good, scores, NEGATIVE) - log_sum)
        weight_grad = dot_tt(grad, value)
        score_grad = (weights * (weight_grad - centre)).astype(BF16)
        total[...] += dot(score_grad, key)
        dkv_ref[here, :HD] = (dot_nt(score_grad, query) * score_scale).astype(BF16)
        dkv_ref[here, HD:] = dot_nt(weights.astype(BF16), grad).astype(BF16)

    def nothing(j):
        dkv_ref[j * rows : (j + 1) * rows, :] = jnp.zeros((rows, 2 * HD), BF16)

    for j in range(groups):
        alive = j * rows < length
        pl.when((j < me) & alive)(functools.partial(block, j, False))
        pl.when((j == me) & alive)(functools.partial(block, j, True))
        pl.when((j > me) | jnp.logical_not(alive))(functools.partial(nothing, j))
    dq_ref[...] = total[...] * score_scale


def attend_back(place, query, grad, out, log_sums, kv, heads, score_scale):
    rows = query.shape[0]
    groups = kv.shape[0] // rows
    head = pl.BlockSpec((rows, HD), lambda h, p: (0, h))
    pair = pl.BlockSpec((groups * rows, 2 * HD), lambda h, p: (0, h))
    spec = pltpu.PrefetchScalarGridSpec(
        num_scalar_prefetch=1,
        grid=(heads,),
        in_specs=[head, head, head, pl.BlockSpec((1, rows, 1), lambda h, p: (h, 0, 0)), pair],
        out_specs=[head, pair],
        scratch_shapes=[pltpu.VMEM((rows, HD), F32)],
    )
    work = heads * rows * rows * groups
    return pl.pallas_call(
        functools.partial(attend_back_kernel, groups=groups, score_scale=score_scale),
        grid_spec=spec,
        out_shape=[
            jax.ShapeDtypeStruct((rows, heads * HD), F32),
            jax.ShapeDtypeStruct((groups * rows, 2 * heads * HD), BF16),
        ],
        compiler_params=pltpu.CompilerParams(vmem_limit_bytes=48 << 20),
        cost_estimate=QUICK,
    )(place, query, grad, out, log_sums, kv)


def side_by_side_kernel(place_ref, *refs, groups):
    pieces, stack, outs = refs[:groups], refs[-1], refs[groups:-1]
    units = pieces[0].shape[1]
    for s in range(groups):
        stack[s] = pieces[s][...]
    for j in range(groups):
        found = stack[place_ref[0] ^ j]
        for i, out in enumerate(outs):
            out[:, j * units : (j + 1) * units] = found[i].astype(F32).T


def side_by_side(place, pieces):
    count, units, rows = pieces[0].shape
    groups = len(pieces)
    return pl.pallas_call(
        functools.partial(side_by_side_kernel, groups=groups),
        grid_spec=pltpu.PrefetchScalarGridSpec(
            num_scalar_prefetch=1,
            in_specs=[pl.BlockSpec(memory_space=pltpu.VMEM)] * groups,
            out_specs=[pl.BlockSpec(memory_space=pltpu.VMEM)] * count,
            scratch_shapes=[pltpu.VMEM((groups, count, units, rows), BF16)],
        ),
        out_shape=[jax.ShapeDtypeStruct((rows, groups * units), F32)] * count,
        compiler_params=pltpu.CompilerParams(vmem_limit_bytes=40 << 20),
    )(place, *pieces)


def mixture_kernel(
    mix_ref, hidden_grad_ref, kept_ref, spot_ref, router_ref, weight_ref,
    lin_grad_ref, hidden_ref, small_ref, part_ref,
    total, probs_ref, logits_ref, gate_grad_ref, *, experts, local,
):
    step = pl.program_id(1)
    width = hidden_ref.shape[1]
    mix = mix_ref[...]
    lane = lax.broadcasted_iota(jnp.int32, kept_ref.shape, 1)

    @pl.when(step == 0)
    def _():
        logits = dot_tt(mix, router_ref[...])
        logits_ref[...] = logits
        masked = jnp.where(lane < experts, logits, NEGATIVE)
        lifted = jnp.exp(masked - jnp.max(masked, axis=1, keepdims=True))
        probs_ref[...] = lifted / jnp.sum(lifted, axis=1, keepdims=True)
        gate_grad_ref[...] = jnp.zeros_like(gate_grad_ref)
        total[...] = jnp.zeros_like(total)

    spot = spot_ref[pl.ds(step, 1), :]
    kept = kept_ref[...].astype(F32)
    gate = jnp.sum(probs_ref[...] * kept * spot, axis=1, keepdims=True)
    switch = jax.nn.sigmoid(jnp.sum(logits_ref[...] * spot, axis=1, keepdims=True))
    routed = step < local
    scale = jnp.where(routed, gate, switch)
    weight = weight_ref[...]
    lin = dot_tt(mix, weight)
    gate_lin, up_lin = lin[:, :width], lin[:, width:]
    logistic = jax.nn.sigmoid(gate_lin)
    silu = gate_lin * logistic
    hidden = silu * up_lin
    hidden_grad = hidden_grad_ref[...]
    row_sum = jnp.sum(hidden * hidden_grad, axis=1, keepdims=True)
    factor = jnp.where(routed, jnp.sum(kept * spot, axis=1, keepdims=True), switch * (1.0 - switch))
    gate_grad_ref[...] += row_sum * factor * spot
    hidden_ref[...] = (scale * hidden).astype(BF16)
    scaled = scale * hidden_grad
    lin_grad_ref[:, :width] = (
        scaled * up_lin * logistic * (1.0 + gate_lin * (1.0 - logistic))
    ).astype(BF16)
    lin_grad_ref[:, width:] = (scaled * silu).astype(BF16)
    total[...] += dot(lin_grad_ref[...], weight)

    @pl.when(step == local)
    def _():
        grads = gate_grad_ref[...]
        probs = probs_ref[...]
        routed_grads = jnp.where(lane < experts, grads, 0.0)
        inner = jnp.sum(probs * routed_grads, axis=1, keepdims=True)
        small = jnp.where(lane < experts, probs * (grads - inner), grads).astype(BF16)
        small_ref[...] = small
        part_ref[...] = (total[...] + dot(small, router_ref[...])).astype(BF16)


def mixture(mix, hidden_grad, kept, spot, router, weight, rows, experts, local):
    tokens, depth = mix.shape
    steps = local + 1
    pair = weight.shape[0] // steps
    width = pair // 2
    whole = lambda shape: pl.BlockSpec(shape, lambda i, j: (0, 0))
    by_row = lambda size: pl.BlockSpec((rows, size), lambda i, j: (i, 0))
    by_both = lambda size: pl.BlockSpec((rows, size), lambda i, j: (i, j))
    return pl.pallas_call(
        functools.partial(mixture_kernel, experts=experts, local=local),
        grid=(tokens // rows, steps),
        in_specs=[
            by_row(depth),
            by_both(width),
            by_row(LANES),
            whole(spot.shape),
            whole((LANES, depth)),
            pl.BlockSpec((pair, depth), lambda i, j: (j, 0)),
        ],
        out_specs=[by_both(pair), by_both(width), by_row(LANES), by_row(depth)],
        out_shape=[
            jax.ShapeDtypeStruct((tokens, steps * pair), BF16),
            jax.ShapeDtypeStruct((tokens, steps * width), BF16),
            jax.ShapeDtypeStruct((tokens, LANES), BF16),
            jax.ShapeDtypeStruct((tokens, depth), BF16),
        ],
        scratch_shapes=[
            pltpu.VMEM((rows, depth), F32),
            pltpu.VMEM((rows, LANES), F32),
            pltpu.VMEM((rows, LANES), F32),
            pltpu.VMEM((rows, LANES), F32),
        ],
        compiler_params=pltpu.CompilerParams(vmem_limit_bytes=56 << 20),
        cost_estimate=pl.CostEstimate(
            flops=5 * tokens * depth * steps * pair, bytes_accessed=80 << 20, transcendentals=0
        ),
    )(mix, hidden_grad, kept, spot, router, weight)


def shards(
    layer_input,
    attention_gain,
    query_weight,
    key_weight,
    value_weight,
    query_bias,
    key_bias,
    value_bias,
    output_weight,
    mixture_gain,
    router_weight,
    expert_gate,
    expert_up,
    expert_down,
    shared_gate,
    shared_up,
    shared_down,
    shared_switch,
    slot_lengths,
    routes,
    cotangent,
):
    rows, depth = layer_input.shape[1:]
    groups = lax.axis_size("expert")
    tensors = lax.axis_size("tensor")
    slots = lax.axis_size("dp")
    slot_at = lax.axis_index("dp")
    block_at = lax.axis_index("expert")
    tensor_at = lax.axis_index("tensor")
    experts = router_weight.shape[1]
    local, _, expert_units = expert_gate.shape
    shared_units = shared_gate.shape[1] // groups
    capacity = rows * TOP // experts
    score_scale = HD ** (-0.5)
    heads_here = query_weight.shape[1] // HD
    wide = heads_here * HD
    piece = rows // tensors
    width = up_to(max(expert_units, shared_units), LANES)
    pair = 2 * width
    steps = local + 1
    length = slot_lengths[0]
    positions = block_at * rows + jnp.arange(rows, dtype=jnp.int32)
    live_rows = positions < length
    place = jnp.stack([block_at.astype(jnp.int32), length])

    links = Links()
    order = reversed_order(groups)
    behind = [(tensor_at - k) % tensors for k in range(tensors)]
    ahead = [(tensor_at + k) % tensors for k in range(tensors)]

    def rows_of(value, index):
        return rows_at(value, index * piece, piece)

    qkv_full = lax.all_gather(
        jnp.concatenate([query_weight, key_weight, value_weight], axis=1),
        ("dp", "expert"), axis=0, tiled=True,
    )
    inputs = layer_input[0].astype(F32)
    gain_one = attention_gain.astype(F32)
    inverse_one = lax.rsqrt(jnp.mean(inputs * inputs, axis=1, keepdims=True) + EPS)
    normed = (inputs * inverse_one * gain_one).astype(BF16)
    bias = jnp.concatenate([query_bias, key_bias, value_bias])[None, :]
    cosine_table, sine_table = rotary_tables(positions, HD)
    queries, kv_own = project(normed, qkv_full, bias, cosine_table, sine_table)
    kv = lax.all_gather(kv_own, "expert", axis=0, tiled=True)
    output_here = lax.all_gather(
        after(output_weight, kv), ("dp", "expert"), axis=0, tiled=True
    )
    heads_low, log_sums = attend(place, queries, kv, heads_here, score_scale)

    (
        route_block, upstream_source, gate_source, up_source, down_source, shared_source, small_source,
    ) = after(
        (
            routes[0], cotangent[0], expert_gate, expert_up, expert_down,
            (shared_gate, shared_up, shared_down), (router_weight, shared_switch),
        ),
        kv_own,
    )

    shared_own = jnp.stack([w.T for w in shared_source])
    own_rows = shared_own.shape[2]

    def units_of(block):
        return lax.dynamic_slice_in_dim(shared_own, block * shared_units, shared_units, axis=1)

    shared_pieces = links.swaps([after(units_of(block_at ^ s), kv) for s in range(1, groups)], "expert")

    expert_ids = jnp.arange(experts, dtype=jnp.int32)
    chosen = jnp.any(route_block[:, :, None] == expert_ids[None, None, :], axis=1) & live_rows[:, None]
    row_ids = jnp.arange(rows, dtype=jnp.int32)
    earlier = (row_ids[None, :] < row_ids[:, None]).astype(BF16)
    before = dot(earlier, chosen.astype(BF16))
    kept = chosen & (before < capacity)
    kept = jnp.pad(kept.astype(BF16), ((0, 0), (0, LANES - experts)))

    upstream_low = jnp.where(live_rows[:, None], upstream_source, jnp.zeros((), BF16))
    upstream_all = links.spread(upstream_low, "expert", low=2)
    kept_all = links.spread(kept, "expert", low=2)

    def pad_units(weight):
        return jnp.pad(weight, ((0, width - weight.shape[0]), (0, 0)))

    gates_t, ups_t, downs_t = (w.transpose(0, 2, 1) for w in (gate_source, up_source, down_source))
    weight_parts = []
    for j in range(local):
        weight_parts += [pad_units(gates_t[j]), pad_units(ups_t[j])]
    lin_weight = jnp.concatenate(weight_parts + [jnp.zeros((pair, depth), BF16)], axis=0)
    down_weight = jnp.concatenate(
        [pad_units(downs_t[j]) for j in range(local)] + [jnp.zeros((width, depth), BF16)], axis=0
    )
    small_weight = jnp.pad(
        jnp.concatenate([small_source[0].T, small_source[1][None, :]], axis=0),
        ((0, LANES - experts - 1), (0, 0)),
    )
    spot_at = jnp.concatenate(
        [block_at * local + jnp.arange(local, dtype=jnp.int32), jnp.full((1,), experts, jnp.int32)]
    )
    spot = (spot_at[:, None] == jnp.arange(LANES, dtype=jnp.int32)[None, :]).astype(F32)
    spot = jnp.pad(spot, ((0, up_to(steps, 8) - steps), (0, 0)))

    shared_pieces = [units_of(block_at)] + shared_pieces
    attended_part = dot_tt(after(heads_low, tuple(shared_pieces)), output_here).astype(BF16)
    shared_half = in_order(shared_pieces, [block_at ^ s for s in range(groups)], 2)
    halves = [shared_half] + links.shifts([shared_half] * (slots - 1), "dp")
    attended = lax.psum_scatter(attended_part, "tensor", scatter_dimension=0, tiled=True).astype(F32)
    inputs_own = rows_of(inputs, tensor_at)
    live_own = rows_of(live_rows, tensor_at)[:, None]
    residual = inputs_own + after(attended, (tuple(halves), upstream_all, kept_all))
    gain_two = mixture_gain.astype(F32)
    inverse_two = lax.rsqrt(jnp.mean(residual * residual, axis=1, keepdims=True) + EPS)
    mix_own = (residual * inverse_two * gain_two).astype(BF16)

    mix_all = lax.all_gather(mix_own, ("expert", "tensor"), axis=0, tiled=True)

    def all_blocks(half):
        found = jnp.concatenate([half, links.swap(half, "expert", 1)], axis=0)
        return in_order(
            [found[i * rows : (i + 1) * rows] for i in range(groups)], [block_at ^ s for s in order], 0
        )

    upstream_all, kept_all = (all_blocks(v) for v in after((upstream_all, kept_all), mix_own))

    halves = list(after(tuple(halves), mix_own))
    for k, found in enumerate(halves):
        column = (slot_at - k) % slots * (depth // slots)
        down_weight = lax.dynamic_update_slice(down_weight, found[2], (local * width, column))
        for i in (0, 1):
            lin_weight = lax.dynamic_update_slice(
                lin_weight, found[i], (local * pair + i * width, column)
            )
    hidden_grads = dot_tt(upstream_all, down_weight)

    output_full = lax.all_gather(
        after(output_weight, (mix_all, hidden_grads)), ("dp", "expert", "tensor"), axis=0, tiled=True
    )
    lin_grads, hiddens, smalls, mix_part = mixture(
        after(mix_all, hidden_grads), hidden_grads, kept_all, spot, small_weight, lin_weight,
        rows, experts, local,
    )
    mix_sum = lax.psum_scatter(after(mix_part, output_full), ("expert", "tensor"), scatter_dimension=0, tiled=True)

    expert_rows = local * width
    down_grad = dot_nt(hiddens[:, :expert_rows], upstream_all).astype(BF16)

    def over_slots(part):
        return links.shifts([part] * (slots - 1), "dp")

    def total(own, arrived):
        return sum((a.astype(F32) for a in arrived), own.astype(F32))

    everyone = ("expert", "dp", "tensor")
    down_parts = jnp.concatenate(
        [down_grad[j * width : j * width + expert_units] for j in range(local)], axis=0
    )
    down_arrived = over_slots(down_parts)

    shared_lin_grad = dot_nt(lin_grads[:, local * pair :], mix_all).astype(BF16)
    shared_down_grad = dot_nt(hiddens[:, expert_rows:], after(upstream_all, down_parts)).astype(BF16)
    shared_part = jnp.concatenate(
        [
            shared_lin_grad[:shared_units],
            shared_lin_grad[width : width + shared_units],
            shared_down_grad[:shared_units],
        ],
        axis=0,
    )
    half = depth // slots

    def half_of(value, index):
        return lax.dynamic_slice_in_dim(value, index * half, half, axis=1)

    lin_parts = []
    for j in range(local):
        found = dot_nt(after(lin_grads[:, j * pair : (j + 1) * pair], shared_part), mix_all).astype(BF16)
        lin_parts.append(
            jnp.concatenate([found[:expert_units], found[width : width + expert_units]], axis=0)
        )
    lin_part = jnp.concatenate(lin_parts, axis=0)
    shared_halves = [half_of(shared_part, (slot_at + k) % slots) for k in range(1, slots)]
    ring = [[(i, (i + k) % slots) for i in range(slots)] for k in range(1, slots)]
    arrived = links.send("x", shared_halves + [lin_part] * (slots - 1), "dp", ring * 2)
    shared_arrived, lin_arrived = arrived[: slots - 1], arrived[slots - 1 :]
    small_grad = dot_nt(after(smalls, down_parts), mix_all)[: experts + 1]
    small_total = sum_over_all(small_grad.reshape(-1), everyone).reshape(experts + 1, depth)

    output_part = dot(after(hiddens, down_parts), down_weight).astype(BF16)
    output_part = output_part.reshape(groups, rows, depth)

    output_full = output_full.reshape(slots * groups, tensors, depth // (slots * groups), wide)
    output_full = output_full.transpose(0, 2, 1, 3).reshape(depth, tensors * wide)
    mix_sum, output_part, lin_own, shared_own_part, output_full = together(
        after(mix_sum, (tuple(down_arrived), small_grad)), output_part, lin_part, shared_part, output_full
    )
    mix_grad = mix_sum.astype(F32)
    down_total = total(down_parts, after(tuple(down_arrived), mix_sum))
    down_total = down_total.reshape(local, expert_units, depth)
    scaled_two = mix_grad * gain_two
    mixture_gain_grad = jnp.sum(mix_grad * residual * inverse_two, axis=0)
    upstream_own = rows_of(upstream_low, tensor_at).astype(F32)
    residual_grad = (
        upstream_own
        + inverse_two * scaled_two
        - residual * inverse_two**3 * jnp.mean(scaled_two * residual, axis=1, keepdims=True)
    )
    attended_grad = residual_grad.astype(BF16)
    attended_all = lax.all_gather(attended_grad, "tensor", axis=0, tiled=True)
    heads_grad_rows = dot(attended_grad, output_full).astype(BF16)

    def heads_of(index):
        return lax.dynamic_slice_in_dim(heads_grad_rows, index * wide, wide, axis=1)

    grads_in = [heads_of(tensor_at)] + links.shifts(
        [heads_of(ahead[k]) for k in range(1, tensors)], "tensor"
    )

    heads_grad = in_order(grads_in, behind, 0)
    query_grads, kv_grads = attend_back(
        place, queries, heads_grad, heads_low, log_sums, kv, heads_here, score_scale
    )
    kv_sum = lax.psum_scatter(kv_grads, "expert", scatter_dimension=0, tiled=True)
    pre_grad, bias_grad = turn_back(
        query_grads, kv_sum, cosine_table, sine_table)
    normed_part = dot_tt(pre_grad, qkv_full).astype(BF16)
    normed_sum = lax.psum_scatter(normed_part, "tensor", scatter_dimension=0, tiled=True)
    normed_grad = after(normed_sum, tuple(arrived)).astype(F32)
    inverse_own = rows_of(inverse_one, tensor_at)
    scaled_one = normed_grad * gain_one
    attention_gain_grad = jnp.sum(normed_grad * inputs_own * inverse_own, axis=0)
    input_grad = (
        residual_grad
        + inverse_own * scaled_one
        - inputs_own * inverse_own**3 * jnp.mean(scaled_one * inputs_own, axis=1, keepdims=True)
    )
    input_low = input_grad.astype(BF16)
    input_all = lax.all_gather(input_low, "tensor", axis=0, tiled=True)

    shared_sum = total(half_of(shared_own_part, slot_at), after(tuple(shared_arrived), input_low))
    shared_sum = shared_sum.astype(BF16).reshape(3, shared_units, depth // slots)
    lin_total = total(lin_own, after(tuple(lin_arrived), input_low))
    lin_total = lin_total.reshape(local, 2, expert_units, depth)

    input_grad = input_all.astype(F32)
    own = depth // (slots * groups)

    def columns_for(value, part):
        return jnp.concatenate(
            [
                lax.dynamic_slice_in_dim(
                    value, (((slot_at + k) % slots) * groups + (block_at ^ s)) * own, own, axis=1
                )
                for s in part
                for k in range(slots)
            ],
            axis=1,
        )

    weight_grads = []
    for part in (order[: groups // 2], order[groups // 2 :]):
        weight_grads.append(
            jnp.concatenate(
                [
                    dot_nt(columns_for(normed, part), after(pre_grad, normed_part)).astype(BF16),
                    dot_nt(columns_for(attended_all, part), heads_low).astype(BF16),
                ],
                axis=1,
            )
        )

    output_part = links.scatter(output_part, "expert", kv_sum)
    mine = [rows_of(output_part, tensor_at)] + links.shifts(
        [rows_of(output_part, ahead[k]) for k in range(1, tensors)], "tensor"
    )
    mixed = sum(s.astype(F32) for s in after(tuple(mine), input_low))
    output_own = jnp.where(live_own, residual + mixed, 0.0).astype(BF16)
    layer_output = lax.all_gather(after(output_own, input_all), "tensor", axis=0, tiled=True)

    weight_grad = links.collect(*weight_grads, "expert")
    weight_grads = [weight_grad[k * own : (k + 1) * own] for k in range(slots)]
    weight_grad = sum(
        p.astype(F32) for p in [weight_grads[0]] + links.shifts(weight_grads[1:], "dp")
    )

    def owned_by(block):
        return lax.dynamic_slice_in_dim(shared_sum, block * own_rows, own_rows, axis=2)

    shared_back = [owned_by(block_at)] + [
        links.swap(owned_by(block_at ^ s), "expert", s) for s in range(1, groups)
    ]
    shared_grads = side_by_side(place, shared_back)

    bias_place = lax.dynamic_update_slice_in_dim(
        jnp.zeros((tensors * 3 * wide,), F32), bias_grad[0], tensor_at * 3 * wide, axis=0
    )
    last_sums = sum_over_all(
        jnp.concatenate([attention_gain_grad, mixture_gain_grad, bias_place]), everyone
    )
    bias_total = lax.dynamic_slice_in_dim(
        last_sums, 2 * depth + tensor_at * 3 * wide, 3 * wide, axis=0
    )
    return (
        layer_output[None],
        input_grad[None],
        last_sums[:depth],
        weight_grad[:, :wide],
        weight_grad[:, wide : 2 * wide],
        weight_grad[:, 2 * wide : 3 * wide],
        bias_total[:wide],
        bias_total[wide : 2 * wide],
        bias_total[2 * wide :],
        weight_grad[:, 3 * wide :],
        last_sums[depth : 2 * depth],
        small_total[:experts].T,
        lin_total[:, 0].transpose(0, 2, 1),
        lin_total[:, 1].transpose(0, 2, 1),
        down_total.transpose(0, 2, 1),
        shared_grads[0],
        shared_grads[1],
        shared_grads[2],
        small_total[experts],
    )


def solution(mesh):
    dense = P(("dp", "expert"), "tensor")
    routed = P("expert", None, "tensor")
    rows = P("dp", "expert", None)
    in_specs = (
        rows, P(), dense, dense, dense, P("tensor"), P("tensor"), P("tensor"), dense, P(), P(),
        routed, routed, routed, dense, dense, dense, P(), P("dp"), rows, rows,
    )
    out_specs = (
        rows, rows, P(), dense, dense, dense, P("tensor"), P("tensor"), P("tensor"), dense, P(), P(),
        routed, routed, routed, dense, dense, dense, P(),
    )
    return jax.shard_map(shards, mesh=mesh, in_specs=in_specs, out_specs=out_specs, check_vma=False)
```

```python
import functools

import jax
import jax.numpy as jnp
from jax import lax
from jax.experimental import pallas as pl
from jax.experimental.pallas import tpu as pltpu
from jax.sharding import PartitionSpec as P

HD = 128
TOP = 4
LANES = 128

EPS = 1e-06
ROPE_BASE = 1000000.0
NEGATIVE = -1e30
F32 = jnp.float32
QUICK = pl.CostEstimate(flops=0, bytes_accessed=1 << 20, transcendentals=0)
BF16 = jnp.bfloat16


def up_to(value, multiple):
    return -(-value // multiple) * multiple


def rotary_tables(positions, head_size):
    half_size = head_size // 2
    exponent = 2.0 * jnp.arange(half_size, dtype=F32) / head_size
    inverse = ROPE_BASE ** (-exponent)
    angles = positions.astype(F32)[:, None] * inverse[None, :]
    cosine_half = jnp.cos(angles)
    sine_half = jnp.sin(angles)
    return (
        jnp.concatenate([cosine_half, cosine_half], axis=1),
        jnp.concatenate([-sine_half, sine_half], axis=1),
    )


class Links:
    def __init__(self):
        self.last = {}

    def send(self, link, values, axis, perms):
        before = None if link == "core" else self.last.get(link)
        if before is not None:
            tied = lax.optimization_barrier((tuple(values), before))
            values = tied[0]
        with jax.named_scope("over_" + link):
            arrived = tuple(lax.ppermute(v, axis, p) for v, p in zip(values, perms))
        self.last[link] = arrived
        return list(arrived)

    def swap(self, value, axis, bit):
        link = "x" if axis == "dp" else "core" if bit == 1 else "y"
        size = lax.axis_size(axis)
        return self.send(link, [value], axis, [[(i, i ^ bit) for i in range(size)]])[0]

    def swaps(self, values, axis):
        size = lax.axis_size(axis)
        perms = [[(i, i ^ s) for i in range(size)] for s in range(1, size)]
        return self.send("y", values, axis, perms)

    def shift(self, value, axis, by):
        size = lax.axis_size(axis)
        perm = [(i, (i + by) % size) for i in range(size)]
        return self.send("x" if axis == "dp" else "z", [value], axis, [perm])[0]

    def shifts(self, values, axis, direction=1):
        link = "x" if axis == "dp" else "z"
        size = lax.axis_size(axis)
        perms = [[(i, (i + direction * k) % size) for i in range(size)] for k in range(1, size)]
        return self.send(link, values, axis, perms[: len(values)])

    def spread(self, value, axis, low=1):
        bit = lax.axis_size(axis) // 2
        while bit >= low:
            value = jnp.concatenate([value, self.swap(value, axis, bit)], axis=0)
            bit //= 2
        return value

    def meet(self, near, far, axis, bit):
        arrived = self.swap(far, axis, bit)
        return (near.astype(F32) + arrived.astype(F32)).astype(near.dtype)

    def scatter(self, value, axis, bit, upto):
        at = lax.axis_index(axis)
        while bit < upto:
            value = value.reshape(value.shape[0] // 2, 2, *value.shape[1:])
            own = lax.rem(at // bit, 2)
            near, far = (
                lax.dynamic_index_in_dim(value, i, axis=1, keepdims=False) for i in (own, 1 - own)
            )
            value = self.meet(near, far, axis, bit)
            bit *= 2
        return value

    def collect(self, near, far, axis, low=1):
        bit = low
        while True:
            arrived = self.swap(far, axis, bit)
            near = (near.astype(F32) + arrived.astype(F32)).astype(near.dtype)
            bit *= 2
            if bit >= lax.axis_size(axis):
                return near
            half = near.shape[0] // 2
            near, far = near[:half], near[half:]


def sum_over_all(value, axes):
    for axis in axes:
        size = lax.axis_size(axis)
        bit = 1
        while bit < size:
            value = value + lax.ppermute(value, axis, [(i, i ^ bit) for i in range(size)])
            bit *= 2
    return value


def reversed_order(size):
    order, bit = [0], size // 2
    while bit:
        order = order + [i ^ bit for i in order]
        bit //= 2
    return order


def after(value, *others):
    return lax.optimization_barrier((value, others))[0]


def together(*values):
    return lax.optimization_barrier(values)


def halves_of(value):
    half = value.shape[0] // 2
    return value[:half], value[half:]


def rows_at(value, start, size):
    return lax.dynamic_slice_in_dim(value, start, size, axis=0)


def in_order(pieces, index, axis):
    size = pieces[0].shape[axis]
    shape = list(pieces[0].shape)
    shape[axis] = size * len(pieces)
    whole = jnp.zeros(shape, pieces[0].dtype)
    for piece, place in zip(pieces, index):
        whole = lax.dynamic_update_slice_in_dim(whole, piece, place * size, axis)
    return whole


def dot_tt(a, b):
    return lax.dot_general(a, b, (((1,), (1,)), ((), ())), preferred_element_type=F32)


def dot_nt(a, b):
    return lax.dot_general(a, b, (((0,), (0,)), ((), ())), preferred_element_type=F32)


def dot(a, b):
    return jnp.dot(a, b, preferred_element_type=F32)


def project_kernel(
    rows_ref, wq_ref, wk_ref, wv_ref, bq_ref, bk_ref, bv_ref, cosine_ref, sine_ref, q_ref, kv_ref
):
    source = rows_ref[...]
    cosine, sine = cosine_ref[...], sine_ref[...]

    def turned(value):
        return value * cosine + pltpu.roll(value, HD // 2, 1) * sine

    query = dot(source, wq_ref[...]) + bq_ref[...].astype(F32)
    key = dot(source, wk_ref[...]) + bk_ref[...].astype(F32)
    value = dot(source, wv_ref[...]) + bv_ref[...].astype(F32)
    for i in range(q_ref.shape[1] // HD):
        here = slice(i * HD, (i + 1) * HD)
        q_ref[:, here] = turned(query[:, here]).astype(BF16)
        kv_ref[:, 2 * i * HD : (2 * i + 1) * HD] = turned(key[:, here]).astype(BF16)
        kv_ref[:, (2 * i + 1) * HD : (2 * i + 2) * HD] = value[:, here].astype(BF16)


def project(source, weight, bias, cosine, sine):
    rows, depth = source.shape
    wide = weight.shape[1] // 3
    block = 2 * HD
    steps = wide // block
    whole = lambda shape: pl.BlockSpec(shape, lambda h: (0, 0))
    third = lambda size, i: pl.BlockSpec((size, block), lambda h: (0, i * steps + h))
    return pl.pallas_call(
        project_kernel,
        grid=(steps,),
        in_specs=[whole((rows, depth))]
        + [third(depth, i) for i in range(3)]
        + [third(1, i) for i in range(3)]
        + [whole((rows, HD))] * 2,
        out_specs=[
            pl.BlockSpec((rows, block), lambda h: (0, h)),
            pl.BlockSpec((rows, 2 * block), lambda h: (0, h)),
        ],
        out_shape=[
            jax.ShapeDtypeStruct((rows, wide), BF16),
            jax.ShapeDtypeStruct((rows, 2 * wide), BF16),
        ],
        compiler_params=pltpu.CompilerParams(vmem_limit_bytes=40 << 20),
        cost_estimate=QUICK,
    )(source, weight, weight, weight, bias, bias, bias, cosine, sine)


def turn_back_kernel(dq_ref, dkv_ref, cosine_ref, sine_ref, out_ref, sum_ref):
    cosine, sine = cosine_ref[...], sine_ref[...]
    wide = dq_ref.shape[1]

    def turned(value):
        return value * cosine - pltpu.roll(value, HD // 2, 1) * sine

    def store(at, value):
        low = value.astype(BF16)
        out_ref[:, at : at + HD] = low
        sum_ref[:, at : at + HD] = jnp.sum(low.astype(F32), axis=0, keepdims=True)

    for i in range(wide // HD):
        at = i * HD
        store(at, turned(dq_ref[:, at : at + HD]))
        here, there = slice(2 * at, 2 * at + HD), slice(2 * at + HD, 2 * at + 2 * HD)
        store(wide + at, turned(dkv_ref[:, here].astype(F32)))
        store(2 * wide + at, dkv_ref[:, there].astype(F32))


def turn_back(query_grads, kv_grads, cosine, sine):
    rows, wide = query_grads.shape
    return pl.pallas_call(
        turn_back_kernel,
        out_shape=[
            jax.ShapeDtypeStruct((rows, 3 * wide), BF16),
            jax.ShapeDtypeStruct((1, 3 * wide), F32),
        ],
        compiler_params=pltpu.CompilerParams(vmem_limit_bytes=40 << 20),
        cost_estimate=QUICK,
    )(query_grads, kv_grads, cosine, sine)


def seen_scores(query, key, length, score_scale):
    rows, columns = query.shape[0], key.shape[0]
    scores = dot_tt(query, key) * score_scale
    column = lax.broadcasted_iota(jnp.int32, (1, columns), 1)
    scores = scores + jnp.where(column < length, 0.0, NEGATIVE)
    far = lax.broadcasted_iota(jnp.int32, (rows, rows), 1) <= lax.broadcasted_iota(jnp.int32, (rows, rows), 0)
    near = jnp.where(far, scores[:, columns - rows :], NEGATIVE)
    return near if columns == rows else jnp.concatenate([scores[:, : columns - rows], near], axis=1)


def attend_kernel(place_ref, q_ref, kv_ref, out_ref, log_ref, *, groups, score_scale):
    me, length = place_ref[0], place_ref[1]
    rows = q_ref.shape[0]
    part = rows // 2

    def block(j):
        for first in range(0, rows, part):
            here, seen = slice(first, first + part), slice(0, j * rows + first + part)
            scores = seen_scores(q_ref[here, :], kv_ref[seen, :HD], length, score_scale)
            peak = jnp.max(scores, axis=1, keepdims=True)
            lifted = jnp.exp(scores - peak)
            total = jnp.sum(lifted, axis=1, keepdims=True)
            mix = dot(lifted.astype(BF16), kv_ref[seen, HD:])
            out_ref[here, :] = (mix / total).astype(BF16)
            log_ref[0, here, :] = peak + jnp.log(total)

    for j in range(groups):
        pl.when(me == j)(functools.partial(block, j))


def attend(place, query, kv, heads, score_scale):
    rows = query.shape[0]
    groups = kv.shape[0] // rows
    spec = pltpu.PrefetchScalarGridSpec(
        num_scalar_prefetch=1,
        grid=(heads,),
        in_specs=[
            pl.BlockSpec((rows, HD), lambda h, p: (0, h)),
            pl.BlockSpec((groups * rows, 2 * HD), lambda h, p: (0, h)),
        ],
        out_specs=[
            pl.BlockSpec((rows, HD), lambda h, p: (0, h)),
            pl.BlockSpec((1, rows, 1), lambda h, p: (h, 0, 0)),
        ],
    )
    work = heads * rows * rows * groups
    return pl.pallas_call(
        functools.partial(attend_kernel, groups=groups, score_scale=score_scale),
        grid_spec=spec,
        out_shape=[
            jax.ShapeDtypeStruct((rows, heads * HD), BF16),
            jax.ShapeDtypeStruct((heads, rows, 1), F32),
        ],
        compiler_params=pltpu.CompilerParams(vmem_limit_bytes=40 << 20),
        cost_estimate=QUICK,
    )(place, query, kv)


def attend_back_kernel(
    place_ref, q_ref, g_ref, o_ref, log_ref, kv_ref, dq_ref, dkv_ref, sums, *, groups, score_scale
):
    me, length = place_ref[0], place_ref[1]
    rows = q_ref.shape[0]
    part = rows // 2

    def block(j):
        for first in reversed(range(0, rows, part)):
            here, seen = slice(first, first + part), slice(0, j * rows + first + part)
            query, grad, key = q_ref[here, :], g_ref[here, :], kv_ref[seen, :HD]
            centre = jnp.sum(
                grad.astype(F32) * o_ref[here, :].astype(F32), axis=1, keepdims=True
            )
            scores = seen_scores(query, key, length, score_scale)
            weights = jnp.exp(scores - log_ref[0, here, :])
            weight_grad = dot_tt(grad, kv_ref[seen, HD:])
            score_grad = (weights * (weight_grad - centre)).astype(BF16)
            dq_ref[here, :] = dot(score_grad, key) * score_scale
            key_grad = dot_nt(score_grad, query) * score_scale
            value_grad = dot_nt(weights.astype(BF16), grad)
            if first + part == rows:
                sums[seen, :HD] = key_grad
                sums[seen, HD:] = value_grad
            else:
                sums[seen, :HD] += key_grad
                sums[seen, HD:] += value_grad
        dkv_ref[: (j + 1) * rows, :] = sums[: (j + 1) * rows, :].astype(BF16)
        if j + 1 < groups:
            rest = (groups - 1 - j) * rows
            dkv_ref[(j + 1) * rows :, :] = jnp.zeros((rest, 2 * HD), BF16)

    for j in range(groups):
        pl.when(me == j)(functools.partial(block, j))


def attend_back(place, query, grad, out, log_sums, kv, heads, score_scale):
    rows = query.shape[0]
    groups = kv.shape[0] // rows
    head = pl.BlockSpec((rows, HD), lambda h, p: (0, h))
    pair = pl.BlockSpec((groups * rows, 2 * HD), lambda h, p: (0, h))
    spec = pltpu.PrefetchScalarGridSpec(
        num_scalar_prefetch=1,
        grid=(heads,),
        in_specs=[head, head, head, pl.BlockSpec((1, rows, 1), lambda h, p: (h, 0, 0)), pair],
        out_specs=[head, pair],
        scratch_shapes=[pltpu.VMEM((groups * rows, 2 * HD), F32)],
    )
    work = heads * rows * rows * groups
    return pl.pallas_call(
        functools.partial(attend_back_kernel, groups=groups, score_scale=score_scale),
        grid_spec=spec,
        out_shape=[
            jax.ShapeDtypeStruct((rows, heads * HD), F32),
            jax.ShapeDtypeStruct((groups * rows, 2 * heads * HD), BF16),
        ],
        compiler_params=pltpu.CompilerParams(vmem_limit_bytes=48 << 20),
        cost_estimate=QUICK,
    )(place, query, grad, out, log_sums, kv)


def side_by_side_kernel(place_ref, *refs, groups):
    pieces, stack, outs = refs[:groups], refs[-1], refs[groups:-1]
    units = pieces[0].shape[1]
    for s in range(groups):
        stack[s] = pieces[s][...]
    for j in range(groups):
        found = stack[place_ref[0] ^ j]
        for i, out in enumerate(outs):
            out[:, j * units : (j + 1) * units] = found[i].astype(F32).T


def side_by_side(place, pieces):
    count, units, rows = pieces[0].shape
    groups = len(pieces)
    return pl.pallas_call(
        functools.partial(side_by_side_kernel, groups=groups),
        grid_spec=pltpu.PrefetchScalarGridSpec(
            num_scalar_prefetch=1,
            in_specs=[pl.BlockSpec(memory_space=pltpu.VMEM)] * groups,
            out_specs=[pl.BlockSpec(memory_space=pltpu.VMEM)] * count,
            scratch_shapes=[pltpu.VMEM((groups, count, units, rows), BF16)],
        ),
        out_shape=[jax.ShapeDtypeStruct((rows, groups * units), F32)] * count,
        compiler_params=pltpu.CompilerParams(vmem_limit_bytes=40 << 20),
    )(place, *pieces)


def mixture_kernel(
    mix_ref, hidden_grad_ref, kept_ref, spot_ref, router_ref, weight_ref,
    lin_grad_ref, hidden_ref, small_ref, part_ref, *, experts, local,
):
    pair = weight_ref.shape[0] // (local + 1)
    width = pair // 2
    mix = mix_ref[...]
    lane = lax.broadcasted_iota(jnp.int32, kept_ref.shape, 1)
    logits = dot_tt(mix, router_ref[...])
    masked = jnp.where(lane < experts, logits, NEGATIVE)
    lifted = jnp.exp(masked - jnp.max(masked, axis=1, keepdims=True))
    probs = lifted / jnp.sum(lifted, axis=1, keepdims=True)
    kept = kept_ref[...].astype(F32)
    grads = jnp.zeros(kept_ref.shape, F32)
    for step in range(local + 1):
        spot = spot_ref[step : step + 1, :]
        if step < local:
            factor = jnp.sum(kept * spot, axis=1, keepdims=True)
            scale = jnp.sum(probs * kept * spot, axis=1, keepdims=True)
        else:
            scale = jax.nn.sigmoid(jnp.sum(logits * spot, axis=1, keepdims=True))
            factor = scale * (1.0 - scale)
        at = step * pair
        lin = dot_tt(mix, weight_ref[at : at + pair, :])
        gate_lin, up_lin = lin[:, :width], lin[:, width:]
        logistic = jax.nn.sigmoid(gate_lin)
        silu = gate_lin * logistic
        hidden = silu * up_lin
        hidden_grad = hidden_grad_ref[:, step * width : (step + 1) * width]
        row_sum = jnp.sum(hidden * hidden_grad, axis=1, keepdims=True)
        grads += row_sum * factor * spot
        hidden_ref[:, step * width : (step + 1) * width] = (scale * hidden).astype(BF16)
        scaled = scale * hidden_grad
        lin_grad_ref[:, at : at + width] = (
            scaled * up_lin * (logistic + silu * (1.0 - logistic))
        ).astype(BF16)
        lin_grad_ref[:, at + width : at + pair] = (scaled * silu).astype(BF16)
    routed_grads = jnp.where(lane < experts, grads, 0.0)
    inner = jnp.sum(probs * routed_grads, axis=1, keepdims=True)
    small = jnp.where(lane < experts, probs * (grads - inner), grads).astype(BF16)
    small_ref[...] = small
    part_ref[...] = (
        dot(lin_grad_ref[...], weight_ref[...]) + dot(small, router_ref[...])
    ).astype(BF16)


def mixture(mix, hidden_grad, kept, spot, router, weight, rows, experts, local):
    tokens, depth = mix.shape
    units = weight.shape[0]
    once = lambda shape: pl.BlockSpec(shape, lambda i: (0, 0), pipeline_mode=pl.Buffered(1))
    by_row = lambda size: pl.BlockSpec((rows, size), lambda i: (i, 0))
    return pl.pallas_call(
        functools.partial(mixture_kernel, experts=experts, local=local),
        grid=(tokens // rows,),
        in_specs=[
            by_row(depth),
            by_row(units // 2),
            by_row(LANES),
            once(spot.shape),
            once((LANES, depth)),
            once((units, depth)),
        ],
        out_specs=[by_row(units), by_row(units // 2), by_row(LANES), by_row(depth)],
        out_shape=[
            jax.ShapeDtypeStruct((tokens, units), BF16),
            jax.ShapeDtypeStruct((tokens, units // 2), BF16),
            jax.ShapeDtypeStruct((tokens, LANES), BF16),
            jax.ShapeDtypeStruct((tokens, depth), BF16),
        ],
        compiler_params=pltpu.CompilerParams(vmem_limit_bytes=60 << 20),
        cost_estimate=pl.CostEstimate(
            flops=5 * tokens * depth * units, bytes_accessed=80 << 20, transcendentals=0
        ),
    )(mix, hidden_grad, kept, spot, router, weight)


def shards(
    layer_input,
    attention_gain,
    query_weight,
    key_weight,
    value_weight,
    query_bias,
    key_bias,
    value_bias,
    output_weight,
    mixture_gain,
    router_weight,
    expert_gate,
    expert_up,
    expert_down,
    shared_gate,
    shared_up,
    shared_down,
    shared_switch,
    slot_lengths,
    routes,
    cotangent,
):
    rows, depth = layer_input.shape[1:]
    groups = lax.axis_size("expert")
    tensors = lax.axis_size("tensor")
    slots = lax.axis_size("dp")
    slot_at = lax.axis_index("dp")
    block_at = lax.axis_index("expert")
    tensor_at = lax.axis_index("tensor")
    experts = router_weight.shape[1]
    local, _, expert_units = expert_gate.shape
    shared_units = shared_gate.shape[1] // groups
    capacity = rows * TOP // experts
    score_scale = HD ** (-0.5)
    heads_here = query_weight.shape[1] // HD
    wide = heads_here * HD
    piece = rows // tensors
    width = up_to(max(expert_units, shared_units), LANES)
    pair = 2 * width
    steps = local + 1
    length = slot_lengths[0]
    positions = block_at * rows + jnp.arange(rows, dtype=jnp.int32)
    live_rows = positions < length
    place = jnp.stack([block_at.astype(jnp.int32), length])

    links = Links()
    order = reversed_order(groups)
    behind = [(tensor_at - k) % tensors for k in range(tensors)]
    ahead = [(tensor_at + k) % tensors for k in range(tensors)]

    def rows_of(value, index):
        return rows_at(value, index * piece, piece)

    qkv_full = lax.all_gather(
        jnp.concatenate([query_weight, key_weight, value_weight], axis=1),
        ("dp", "expert"), axis=0, tiled=True,
    )
    inputs = layer_input[0].astype(F32)
    gain_one = attention_gain.astype(F32)
    inverse_one = lax.rsqrt(jnp.mean(inputs * inputs, axis=1, keepdims=True) + EPS)
    normed = (inputs * inverse_one * gain_one).astype(BF16)
    bias = jnp.concatenate([query_bias, key_bias, value_bias])[None, :]
    cosine_table, sine_table = rotary_tables(positions, HD)
    queries, kv_own = project(normed, qkv_full, bias, cosine_table, sine_table)
    kv = lax.all_gather(kv_own, "expert", axis=0, tiled=True)
    output_here = lax.all_gather(
        after(output_weight, kv), ("dp", "expert"), axis=0, tiled=True
    )

    (
        route_block, upstream_source, gate_source, up_source, down_source, shared_source, small_source,
    ) = after(
        (
            routes[0], cotangent[0], expert_gate, expert_up, expert_down,
            (shared_gate, shared_up, shared_down), (router_weight, shared_switch),
        ),
        kv_own,
    )

    shared_own = jnp.stack([w.T for w in shared_source])
    own_rows = shared_own.shape[2]

    def units_of(block):
        return lax.dynamic_slice_in_dim(shared_own, block * shared_units, shared_units, axis=1)

    shared_pieces = links.swaps([after(units_of(block_at ^ s), kv) for s in range(1, groups)], "expert")

    heads_low, log_sums = attend(place, queries, kv, heads_here, score_scale)

    expert_ids = jnp.arange(experts, dtype=jnp.int32)
    chosen = jnp.any(route_block[:, :, None] == expert_ids[None, None, :], axis=1) & live_rows[:, None]
    row_ids = jnp.arange(rows, dtype=jnp.int32)
    earlier = (row_ids[None, :] < row_ids[:, None]).astype(BF16)
    before = dot(earlier, chosen.astype(BF16))
    kept = chosen & (before < capacity)
    kept = jnp.pad(kept.astype(BF16), ((0, 0), (0, LANES - experts)))

    upstream_low = jnp.where(live_rows[:, None], upstream_source, jnp.zeros((), BF16))
    upstream_all = links.spread(upstream_low, "expert", low=2)
    kept_all = links.spread(kept, "expert", low=2)

    def pad_units(weight):
        return jnp.pad(weight, ((0, width - weight.shape[0]), (0, 0)))

    gates_t, ups_t, downs_t = (w.transpose(0, 2, 1) for w in (gate_source, up_source, down_source))
    weight_parts = []
    for j in range(local):
        weight_parts += [pad_units(gates_t[j]), pad_units(ups_t[j])]
    lin_weight = jnp.concatenate(weight_parts + [jnp.zeros((pair, depth), BF16)], axis=0)
    down_weight = jnp.concatenate(
        [pad_units(downs_t[j]) for j in range(local)] + [jnp.zeros((width, depth), BF16)], axis=0
    )
    small_weight = jnp.pad(
        jnp.concatenate([small_source[0].T, small_source[1][None, :]], axis=0),
        ((0, LANES - experts - 1), (0, 0)),
    )
    spot_at = jnp.concatenate(
        [block_at * local + jnp.arange(local, dtype=jnp.int32), jnp.full((1,), experts, jnp.int32)]
    )
    spot = (spot_at[:, None] == jnp.arange(LANES, dtype=jnp.int32)[None, :]).astype(F32)
    spot = jnp.pad(spot, ((0, up_to(steps, 8) - steps), (0, 0)))

    shared_pieces = [units_of(block_at)] + shared_pieces
    attended_part = dot_tt(after(heads_low, tuple(shared_pieces)), output_here).astype(BF16)
    shared_half = in_order(shared_pieces, [block_at ^ s for s in range(groups)], 2)
    halves = [shared_half] + links.shifts([shared_half] * (slots - 1), "dp")
    attended = lax.psum_scatter(attended_part, "tensor", scatter_dimension=0, tiled=True).astype(F32)
    inputs_own = rows_of(inputs, tensor_at)
    live_own = rows_of(live_rows, tensor_at)[:, None]
    residual = inputs_own + after(attended, (tuple(halves), upstream_all, kept_all))
    gain_two = mixture_gain.astype(F32)
    inverse_two = lax.rsqrt(jnp.mean(residual * residual, axis=1, keepdims=True) + EPS)
    mix_own = (residual * inverse_two * gain_two).astype(BF16)

    mix_all = lax.all_gather(mix_own, ("expert", "tensor"), axis=0, tiled=True)

    def all_blocks(half):
        found = jnp.concatenate([half, links.swap(half, "expert", 1)], axis=0)
        return in_order(
            [found[i * rows : (i + 1) * rows] for i in range(groups)], [block_at ^ s for s in order], 0
        )

    upstream_all, kept_all = (all_blocks(v) for v in after((upstream_all, kept_all), mix_own))

    halves = list(after(tuple(halves), mix_own))
    for k, found in enumerate(halves):
        column = (slot_at - k) % slots * (depth // slots)
        down_weight = lax.dynamic_update_slice(down_weight, found[2], (local * width, column))
        for i in (0, 1):
            lin_weight = lax.dynamic_update_slice(
                lin_weight, found[i], (local * pair + i * width, column)
            )
    hidden_grads = dot_tt(upstream_all, down_weight)

    lin_grads, hiddens, smalls, mix_part = mixture(
        after(mix_all, hidden_grads), hidden_grads, kept_all, spot, small_weight, lin_weight,
        rows, experts, local,
    )
    mix_sum = lax.psum_scatter(mix_part, ("expert", "tensor"), scatter_dimension=0, tiled=True)

    expert_rows = local * width
    down_grad = dot_nt(hiddens[:, :expert_rows], upstream_all).astype(BF16)

    def over_slots(part):
        return links.shifts([part] * (slots - 1), "dp")

    def total(own, arrived):
        return sum((a.astype(F32) for a in arrived), own.astype(F32))

    everyone = ("expert", "dp", "tensor")
    down_parts = jnp.concatenate(
        [down_grad[j * width : j * width + expert_units] for j in range(local)], axis=0
    )
    down_arrived = over_slots(down_parts)

    shared_lin_grad = dot_nt(lin_grads[:, local * pair :], mix_all).astype(BF16)
    shared_down_grad = dot_nt(hiddens[:, expert_rows:], after(upstream_all, down_parts)).astype(BF16)
    shared_part = jnp.concatenate(
        [
            shared_lin_grad[:shared_units],
            shared_lin_grad[width : width + shared_units],
            shared_down_grad[:shared_units],
        ],
        axis=0,
    )
    half = depth // slots

    def half_of(value, index):
        return lax.dynamic_slice_in_dim(value, index * half, half, axis=1)

    lin_parts = []
    for j in range(local):
        earlier_ones = (shared_part, tuple(down_arrived)) if j == local - 1 else (shared_part,)
        found = dot_nt(after(lin_grads[:, j * pair : (j + 1) * pair], earlier_ones), mix_all)
        found = found.astype(BF16)
        lin_parts.append(
            jnp.concatenate([found[:expert_units], found[width : width + expert_units]], axis=0)
        )
    shared_arrived = links.shifts(
        [half_of(shared_part, (slot_at + k) % slots) for k in range(1, slots)], "dp"
    )
    lin_arrived = [over_slots(part) for part in lin_parts]
    small_grad = dot_nt(after(smalls, down_parts), mix_all)[: experts + 1]

    output_part = dot(after(hiddens, down_parts), down_weight).astype(BF16)
    output_part = output_part.reshape(groups, rows, depth)

    output_part = links.scatter(output_part, "expert", 1, 2)
    mix_sum, output_part, lin_parts, shared_own_part = together(
        after(mix_sum, small_grad), output_part, tuple(lin_parts), shared_part
    )
    mix_grad = mix_sum.astype(F32)
    down_total = total(down_parts, after(tuple(down_arrived), mix_sum))
    down_total = down_total.reshape(local, expert_units, depth)
    scaled_two = mix_grad * gain_two
    mixture_gain_grad = jnp.sum(mix_grad * residual * inverse_two, axis=0)
    upstream_own = rows_of(upstream_low, tensor_at).astype(F32)
    residual_grad = (
        upstream_own
        + inverse_two * scaled_two
        - residual * inverse_two**3 * jnp.mean(scaled_two * residual, axis=1, keepdims=True)
    )
    attended_grad = residual_grad.astype(BF16)
    attended_all = lax.all_gather(attended_grad, "tensor", axis=0, tiled=True)
    output_part = links.scatter(output_part, "expert", 2, groups)[0]
    attended_all, output_part = together(after(attended_all, tuple(shared_arrived)), output_part)
    heads_grad = dot(attended_all, output_here).astype(BF16)

    mine = [rows_of(output_part, tensor_at)] + links.shifts(
        [rows_of(output_part, ahead[k]) for k in range(1, tensors)], "tensor"
    )
    query_grads, kv_grads = attend_back(
        place, queries, heads_grad, heads_low, log_sums, kv, heads_here, score_scale
    )
    kv_sum = lax.psum_scatter(kv_grads, "expert", scatter_dimension=0, tiled=True)
    pre_grad, bias_grad = turn_back(
        query_grads, after(kv_sum, tuple(mine)), cosine_table, sine_table)
    normed_part = dot_tt(pre_grad, qkv_full).astype(BF16)
    normed_sum = lax.psum_scatter(normed_part, "tensor", scatter_dimension=0, tiled=True)
    normed_grad = normed_sum.astype(F32)
    inverse_own = rows_of(inverse_one, tensor_at)
    scaled_one = normed_grad * gain_one
    attention_gain_grad = jnp.sum(normed_grad * inputs_own * inverse_own, axis=0)
    input_grad = (
        residual_grad
        + inverse_own * scaled_one
        - inputs_own * inverse_own**3 * jnp.mean(scaled_one * inputs_own, axis=1, keepdims=True)
    )
    input_low = input_grad.astype(BF16)
    input_all = lax.all_gather(input_low, "tensor", axis=0, tiled=True)

    shared_sum = total(half_of(shared_own_part, slot_at), after(tuple(shared_arrived), pre_grad))
    shared_sum = shared_sum.astype(BF16).reshape(3, shared_units, depth // slots)
    lin_total = jnp.stack(
        [
            total(part, after(tuple(found), input_low)).reshape(2, expert_units, depth)
            for part, found in zip(lin_parts, lin_arrived)
        ]
    )

    input_grad = input_all.astype(F32)
    own = depth // (slots * groups)

    def columns_for(value, part):
        return jnp.concatenate(
            [
                lax.dynamic_slice_in_dim(
                    value, (((slot_at + k) % slots) * groups + (block_at ^ s)) * own, own, axis=1
                )
                for s in part
                for k in range(slots)
            ],
            axis=1,
        )

    weight_grads = []
    for part in (order[: groups // 2], order[groups // 2 :]):
        weight_grads.append(
            jnp.concatenate(
                [
                    dot_nt(
                        columns_for(normed, part), after(pre_grad, (normed_part, tuple(lin_arrived[0])))
                    ).astype(BF16),
                    dot_nt(columns_for(attended_all, part), heads_low).astype(BF16),
                ],
                axis=1,
            )
        )

    mixed = sum(s.astype(F32) for s in mine)
    output_own = jnp.where(live_own, residual + mixed, 0.0).astype(BF16)
    layer_output = lax.all_gather(after(output_own, input_all), "tensor", axis=0, tiled=True)

    def owned_by(block):
        return lax.dynamic_slice_in_dim(shared_sum, block * own_rows, own_rows, axis=2)

    shared_back = [owned_by(block_at)] + [
        links.swap(owned_by(block_at ^ s), "expert", s) for s in range(1, groups)
    ]
    shared_grads = side_by_side(place, shared_back)

    bias_place = lax.dynamic_update_slice_in_dim(
        jnp.zeros((tensors * 3 * wide,), F32), bias_grad[0], tensor_at * 3 * wide, axis=0
    )
    last_sums = sum_over_all(
        jnp.concatenate(
            [attention_gain_grad, mixture_gain_grad, small_grad.reshape(-1), bias_place]
        ),
        everyone,
    )
    weight_grad = links.meet(weight_grads[0], after(weight_grads[1], input_low), "expert", 1)
    weight_grad = links.collect(*halves_of(weight_grad), "expert", low=2)
    weight_grads = [weight_grad[k * own : (k + 1) * own] for k in range(slots)]
    weight_grad = sum(
        p.astype(F32) for p in [weight_grads[0]] + links.shifts(weight_grads[1:], "dp")
    )

    small_total = last_sums[2 * depth : (3 + experts) * depth].reshape(experts + 1, depth)
    bias_total = lax.dynamic_slice_in_dim(
        last_sums, (3 + experts) * depth + tensor_at * 3 * wide, 3 * wide, axis=0
    )
    return (
        layer_output[None],
        input_grad[None],
        last_sums[:depth],
        weight_grad[:, :wide],
        weight_grad[:, wide : 2 * wide],
        weight_grad[:, 2 * wide : 3 * wide],
        bias_total[:wide],
        bias_total[wide : 2 * wide],
        bias_total[2 * wide :],
        weight_grad[:, 3 * wide :],
        last_sums[depth : 2 * depth],
        small_total[:experts].T,
        lin_total[:, 0].transpose(0, 2, 1),
        lin_total[:, 1].transpose(0, 2, 1),
        down_total.transpose(0, 2, 1),
        shared_grads[0],
        shared_grads[1],
        shared_grads[2],
        small_total[experts],
    )


def solution(mesh):
    dense = P(("dp", "expert"), "tensor")
    routed = P("expert", None, "tensor")
    rows = P("dp", "expert", None)
    in_specs = (
        rows, P(), dense, dense, dense, P("tensor"), P("tensor"), P("tensor"), dense, P(), P(),
        routed, routed, routed, dense, dense, dense, P(), P("dp"), rows, rows,
    )
    out_specs = (
        rows, rows, P(), dense, dense, dense, P("tensor"), P("tensor"), P("tensor"), dense, P(), P(),
        routed, routed, routed, dense, dense, dense, P(),
    )
    return jax.shard_map(shards, mesh=mesh, in_specs=in_specs, out_specs=out_specs, check_vma=False)
```

```python
import functools

import jax
import jax.numpy as jnp
from jax import lax
from jax.experimental import pallas as pl
from jax.experimental.pallas import tpu as pltpu
from jax.sharding import PartitionSpec as P

HD = 128
TOP = 4
LANES = 128

EPS = 1e-06
ROPE_BASE = 1000000.0
NEGATIVE = -1e30
F32 = jnp.float32
QUICK = pl.CostEstimate(flops=0, bytes_accessed=1 << 20, transcendentals=0)
BF16 = jnp.bfloat16


def up_to(value, multiple):
    return -(-value // multiple) * multiple


def rotary_tables(positions, head_size):
    half_size = head_size // 2
    exponent = 2.0 * jnp.arange(half_size, dtype=F32) / head_size
    inverse = ROPE_BASE ** (-exponent)
    angles = positions.astype(F32)[:, None] * inverse[None, :]
    cosine_half = jnp.cos(angles)
    sine_half = jnp.sin(angles)
    return (
        jnp.concatenate([cosine_half, cosine_half], axis=1),
        jnp.concatenate([-sine_half, sine_half], axis=1),
    )


class Links:
    def __init__(self):
        self.last = {}

    def send(self, link, values, axis, perms):
        before = None if link == "core" else self.last.get(link)
        if before is not None:
            tied = lax.optimization_barrier((tuple(values), before))
            values = tied[0]
        with jax.named_scope("over_" + link):
            arrived = tuple(lax.ppermute(v, axis, p) for v, p in zip(values, perms))
        self.last[link] = arrived
        return list(arrived)

    def swap(self, value, axis, bit):
        link = "x" if axis == "dp" else "core" if bit == 1 else "y"
        size = lax.axis_size(axis)
        return self.send(link, [value], axis, [[(i, i ^ bit) for i in range(size)]])[0]

    def swaps(self, values, axis):
        size = lax.axis_size(axis)
        perms = [[(i, i ^ s) for i in range(size)] for s in range(1, size)]
        return self.send("y", values, axis, perms)

    def shift(self, value, axis, by):
        size = lax.axis_size(axis)
        perm = [(i, (i + by) % size) for i in range(size)]
        return self.send("x" if axis == "dp" else "z", [value], axis, [perm])[0]

    def shifts(self, values, axis, direction=1):
        link = "x" if axis == "dp" else "z"
        size = lax.axis_size(axis)
        perms = [[(i, (i + direction * k) % size) for i in range(size)] for k in range(1, size)]
        return self.send(link, values, axis, perms[: len(values)])

    def spread(self, value, axis, low=1):
        bit = lax.axis_size(axis) // 2
        while bit >= low:
            value = jnp.concatenate([value, self.swap(value, axis, bit)], axis=0)
            bit //= 2
        return value

    def meet(self, near, far, axis, bit):
        arrived = self.swap(far, axis, bit)
        return (near.astype(F32) + arrived.astype(F32)).astype(near.dtype)

    def scatter(self, value, axis, bit, upto):
        at = lax.axis_index(axis)
        while bit < upto:
            value = value.reshape(value.shape[0] // 2, 2, *value.shape[1:])
            own = lax.rem(at // bit, 2)
            near, far = (
                lax.dynamic_index_in_dim(value, i, axis=1, keepdims=False) for i in (own, 1 - own)
            )
            value = self.meet(near, far, axis, bit)
            bit *= 2
        return value

    def collect(self, near, far, axis, low=1):
        bit = low
        while True:
            arrived = self.swap(far, axis, bit)
            near = (near.astype(F32) + arrived.astype(F32)).astype(near.dtype)
            bit *= 2
            if bit >= lax.axis_size(axis):
                return near
            half = near.shape[0] // 2
            near, far = near[:half], near[half:]


def sum_over_all(value, axes):
    for axis in axes:
        size = lax.axis_size(axis)
        bit = 1
        while bit < size:
            value = value + lax.ppermute(value, axis, [(i, i ^ bit) for i in range(size)])
            bit *= 2
    return value


def reversed_order(size):
    order, bit = [0], size // 2
    while bit:
        order = order + [i ^ bit for i in order]
        bit //= 2
    return order


def after(value, *others):
    return lax.optimization_barrier((value, others))[0]


def together(*values):
    return lax.optimization_barrier(values)


def halves_of(value):
    half = value.shape[0] // 2
    return value[:half], value[half:]


def rows_at(value, start, size):
    return lax.dynamic_slice_in_dim(value, start, size, axis=0)


def in_order(pieces, index, axis):
    size = pieces[0].shape[axis]
    shape = list(pieces[0].shape)
    shape[axis] = size * len(pieces)
    whole = jnp.zeros(shape, pieces[0].dtype)
    for piece, place in zip(pieces, index):
        whole = lax.dynamic_update_slice_in_dim(whole, piece, place * size, axis)
    return whole


def dot_tt(a, b):
    return lax.dot_general(a, b, (((1,), (1,)), ((), ())), preferred_element_type=F32)


def dot_nt(a, b):
    return lax.dot_general(a, b, (((0,), (0,)), ((), ())), preferred_element_type=F32)


def dot(a, b):
    return jnp.dot(a, b, preferred_element_type=F32)


def project_kernel(
    rows_ref, wq_ref, wk_ref, wv_ref, bq_ref, bk_ref, bv_ref, cosine_ref, sine_ref, q_ref, kv_ref
):
    source = rows_ref[...]
    cosine, sine = cosine_ref[...], sine_ref[...]

    def turned(value):
        return value * cosine + pltpu.roll(value, HD // 2, 1) * sine

    query = dot(source, wq_ref[...]) + bq_ref[...].astype(F32)
    key = dot(source, wk_ref[...]) + bk_ref[...].astype(F32)
    value = dot(source, wv_ref[...]) + bv_ref[...].astype(F32)
    for i in range(q_ref.shape[1] // HD):
        here = slice(i * HD, (i + 1) * HD)
        q_ref[:, here] = turned(query[:, here]).astype(BF16)
        kv_ref[:, 2 * i * HD : (2 * i + 1) * HD] = turned(key[:, here]).astype(BF16)
        kv_ref[:, (2 * i + 1) * HD : (2 * i + 2) * HD] = value[:, here].astype(BF16)


def project(source, weight, bias, cosine, sine):
    rows, depth = source.shape
    wide = weight.shape[1] // 3
    block = 2 * HD
    steps = wide // block
    whole = lambda shape: pl.BlockSpec(shape, lambda h: (0, 0))
    third = lambda size, i: pl.BlockSpec((size, block), lambda h: (0, i * steps + h))
    return pl.pallas_call(
        project_kernel,
        grid=(steps,),
        in_specs=[whole((rows, depth))]
        + [third(depth, i) for i in range(3)]
        + [third(1, i) for i in range(3)]
        + [whole((rows, HD))] * 2,
        out_specs=[
            pl.BlockSpec((rows, block), lambda h: (0, h)),
            pl.BlockSpec((rows, 2 * block), lambda h: (0, h)),
        ],
        out_shape=[
            jax.ShapeDtypeStruct((rows, wide), BF16),
            jax.ShapeDtypeStruct((rows, 2 * wide), BF16),
        ],
        compiler_params=pltpu.CompilerParams(vmem_limit_bytes=40 << 20),
        cost_estimate=QUICK,
    )(source, weight, weight, weight, bias, bias, bias, cosine, sine)


def turn_back_kernel(dq_ref, dkv_ref, cosine_ref, sine_ref, out_ref, sum_ref):
    cosine, sine = cosine_ref[...], sine_ref[...]
    wide = dq_ref.shape[1]

    def turned(value):
        return value * cosine - pltpu.roll(value, HD // 2, 1) * sine

    def store(at, value):
        low = value.astype(BF16)
        out_ref[:, at : at + HD] = low
        sum_ref[:, at : at + HD] = jnp.sum(low.astype(F32), axis=0, keepdims=True)

    for i in range(wide // HD):
        at = i * HD
        store(at, turned(dq_ref[:, at : at + HD]))
        here, there = slice(2 * at, 2 * at + HD), slice(2 * at + HD, 2 * at + 2 * HD)
        store(wide + at, turned(dkv_ref[:, here].astype(F32)))
        store(2 * wide + at, dkv_ref[:, there].astype(F32))


def turn_back(query_grads, kv_grads, cosine, sine):
    rows, wide = query_grads.shape
    return pl.pallas_call(
        turn_back_kernel,
        out_shape=[
            jax.ShapeDtypeStruct((rows, 3 * wide), BF16),
            jax.ShapeDtypeStruct((1, 3 * wide), F32),
        ],
        compiler_params=pltpu.CompilerParams(vmem_limit_bytes=40 << 20),
        cost_estimate=QUICK,
    )(query_grads, kv_grads, cosine, sine)


def seen_scores(query, key, length, score_scale):
    rows, columns = query.shape[0], key.shape[0]
    scores = dot_tt(query, key) * score_scale
    column = lax.broadcasted_iota(jnp.int32, (1, columns), 1)
    scores = scores + jnp.where(column < length, 0.0, NEGATIVE)
    far = lax.broadcasted_iota(jnp.int32, (rows, rows), 1) <= lax.broadcasted_iota(jnp.int32, (rows, rows), 0)
    near = jnp.where(far, scores[:, columns - rows :], NEGATIVE)
    return near if columns == rows else jnp.concatenate([scores[:, : columns - rows], near], axis=1)


def attend_kernel(place_ref, q_ref, kv_ref, out_ref, log_ref, *, groups, score_scale):
    me, length = place_ref[0], place_ref[1]
    rows = q_ref.shape[0]
    part = rows // 2

    def block(j):
        for first in range(0, rows, part):
            here, seen = slice(first, first + part), slice(0, j * rows + first + part)
            scores = seen_scores(q_ref[here, :], kv_ref[seen, :HD], length, score_scale)
            peak = jnp.max(scores, axis=1, keepdims=True)
            lifted = jnp.exp(scores - peak)
            total = jnp.sum(lifted, axis=1, keepdims=True)
            mix = dot(lifted.astype(BF16), kv_ref[seen, HD:])
            out_ref[here, :] = (mix / total).astype(BF16)
            log_ref[0, here, :] = peak + jnp.log(total)

    for j in range(groups):
        pl.when(me == j)(functools.partial(block, j))


def attend(place, query, kv, heads, score_scale):
    rows = query.shape[0]
    groups = kv.shape[0] // rows
    spec = pltpu.PrefetchScalarGridSpec(
        num_scalar_prefetch=1,
        grid=(heads,),
        in_specs=[
            pl.BlockSpec((rows, HD), lambda h, p: (0, h)),
            pl.BlockSpec((groups * rows, 2 * HD), lambda h, p: (0, h)),
        ],
        out_specs=[
            pl.BlockSpec((rows, HD), lambda h, p: (0, h)),
            pl.BlockSpec((1, rows, 1), lambda h, p: (h, 0, 0)),
        ],
    )
    work = heads * rows * rows * groups
    return pl.pallas_call(
        functools.partial(attend_kernel, groups=groups, score_scale=score_scale),
        grid_spec=spec,
        out_shape=[
            jax.ShapeDtypeStruct((rows, heads * HD), BF16),
            jax.ShapeDtypeStruct((heads, rows, 1), F32),
        ],
        compiler_params=pltpu.CompilerParams(vmem_limit_bytes=40 << 20),
        cost_estimate=QUICK,
    )(place, query, kv)


def attend_back_kernel(
    place_ref, q_ref, g_ref, o_ref, log_ref, kv_ref, dq_ref, dkv_ref, sums, *, groups, score_scale
):
    me, length = place_ref[0], place_ref[1]
    rows = q_ref.shape[0]
    part = rows // 2

    def block(j):
        for first in reversed(range(0, rows, part)):
            here, seen = slice(first, first + part), slice(0, j * rows + first + part)
            query, grad, key = q_ref[here, :], g_ref[here, :], kv_ref[seen, :HD]
            centre = jnp.sum(
                grad.astype(F32) * o_ref[here, :].astype(F32), axis=1, keepdims=True
            )
            scores = seen_scores(query, key, length, score_scale)
            weights = jnp.exp(scores - log_ref[0, here, :])
            weight_grad = dot_tt(grad, kv_ref[seen, HD:])
            score_grad = (weights * (weight_grad - centre)).astype(BF16)
            dq_ref[here, :] = dot(score_grad, key) * score_scale
            key_grad = dot_nt(score_grad, query) * score_scale
            value_grad = dot_nt(weights.astype(BF16), grad)
            if first + part == rows:
                sums[seen, :HD] = key_grad
                sums[seen, HD:] = value_grad
            else:
                sums[seen, :HD] += key_grad
                sums[seen, HD:] += value_grad
        dkv_ref[: (j + 1) * rows, :] = sums[: (j + 1) * rows, :].astype(BF16)
        if j + 1 < groups:
            rest = (groups - 1 - j) * rows
            dkv_ref[(j + 1) * rows :, :] = jnp.zeros((rest, 2 * HD), BF16)

    for j in range(groups):
        pl.when(me == j)(functools.partial(block, j))


def attend_back(place, query, grad, out, log_sums, kv, heads, score_scale):
    rows = query.shape[0]
    groups = kv.shape[0] // rows
    head = pl.BlockSpec((rows, HD), lambda h, p: (0, h))
    pair = pl.BlockSpec((groups * rows, 2 * HD), lambda h, p: (0, h))
    spec = pltpu.PrefetchScalarGridSpec(
        num_scalar_prefetch=1,
        grid=(heads,),
        in_specs=[head, head, head, pl.BlockSpec((1, rows, 1), lambda h, p: (h, 0, 0)), pair],
        out_specs=[head, pair],
        scratch_shapes=[pltpu.VMEM((groups * rows, 2 * HD), F32)],
    )
    work = heads * rows * rows * groups
    return pl.pallas_call(
        functools.partial(attend_back_kernel, groups=groups, score_scale=score_scale),
        grid_spec=spec,
        out_shape=[
            jax.ShapeDtypeStruct((rows, heads * HD), F32),
            jax.ShapeDtypeStruct((groups * rows, 2 * heads * HD), BF16),
        ],
        compiler_params=pltpu.CompilerParams(vmem_limit_bytes=48 << 20),
        cost_estimate=QUICK,
    )(place, query, grad, out, log_sums, kv)


def side_by_side_kernel(place_ref, *refs, groups):
    pieces, stack, outs = refs[:groups], refs[-1], refs[groups:-1]
    units = pieces[0].shape[1]
    for s in range(groups):
        stack[s] = pieces[s][...]
    for j in range(groups):
        found = stack[place_ref[0] ^ j]
        for i, out in enumerate(outs):
            out[:, j * units : (j + 1) * units] = found[i].astype(F32).T


def side_by_side(place, pieces):
    count, units, rows = pieces[0].shape
    groups = len(pieces)
    return pl.pallas_call(
        functools.partial(side_by_side_kernel, groups=groups),
        grid_spec=pltpu.PrefetchScalarGridSpec(
            num_scalar_prefetch=1,
            in_specs=[pl.BlockSpec(memory_space=pltpu.VMEM)] * groups,
            out_specs=[pl.BlockSpec(memory_space=pltpu.VMEM)] * count,
            scratch_shapes=[pltpu.VMEM((groups, count, units, rows), BF16)],
        ),
        out_shape=[jax.ShapeDtypeStruct((rows, groups * units), F32)] * count,
        compiler_params=pltpu.CompilerParams(vmem_limit_bytes=40 << 20),
    )(place, *pieces)


def mixture_kernel(
    mix_ref, hidden_grad_ref, kept_ref, spot_ref, router_ref, weight_ref,
    lin_grad_ref, hidden_ref, small_ref, part_ref, *, experts, local,
):
    pair = weight_ref.shape[0] // (local + 1)
    width = pair // 2
    mix = mix_ref[...]
    lane = lax.broadcasted_iota(jnp.int32, kept_ref.shape, 1)
    logits = dot_tt(mix, router_ref[...])
    masked = jnp.where(lane < experts, logits, NEGATIVE)
    lifted = jnp.exp(masked - jnp.max(masked, axis=1, keepdims=True))
    probs = lifted / jnp.sum(lifted, axis=1, keepdims=True)
    kept = kept_ref[...].astype(F32)
    grads = jnp.zeros(kept_ref.shape, F32)
    for step in range(local + 1):
        spot = spot_ref[step : step + 1, :]
        if step < local:
            factor = jnp.sum(kept * spot, axis=1, keepdims=True)
            scale = jnp.sum(probs * kept * spot, axis=1, keepdims=True)
        else:
            scale = jax.nn.sigmoid(jnp.sum(logits * spot, axis=1, keepdims=True))
            factor = scale * (1.0 - scale)
        at = step * pair
        lin = dot_tt(mix, weight_ref[at : at + pair, :])
        gate_lin, up_lin = lin[:, :width], lin[:, width:]
        logistic = jax.nn.sigmoid(gate_lin)
        silu = gate_lin * logistic
        hidden = silu * up_lin
        hidden_grad = hidden_grad_ref[:, step * width : (step + 1) * width]
        row_sum = jnp.sum(hidden * hidden_grad, axis=1, keepdims=True)
        grads += row_sum * factor * spot
        hidden_ref[:, step * width : (step + 1) * width] = (scale * hidden).astype(BF16)
        scaled = scale * hidden_grad
        lin_grad_ref[:, at : at + width] = (
            scaled * up_lin * (logistic + silu * (1.0 - logistic))
        ).astype(BF16)
        lin_grad_ref[:, at + width : at + pair] = (scaled * silu).astype(BF16)
    routed_grads = jnp.where(lane < experts, grads, 0.0)
    inner = jnp.sum(probs * routed_grads, axis=1, keepdims=True)
    small = jnp.where(lane < experts, probs * (grads - inner), grads).astype(BF16)
    small_ref[...] = small
    part_ref[...] = (
        dot(lin_grad_ref[...], weight_ref[...]) + dot(small, router_ref[...])
    ).astype(BF16)


def mixture(mix, hidden_grad, kept, spot, router, weight, rows, experts, local):
    tokens, depth = mix.shape
    units = weight.shape[0]
    once = lambda shape: pl.BlockSpec(shape, lambda i: (0, 0), pipeline_mode=pl.Buffered(1))
    by_row = lambda size: pl.BlockSpec((rows, size), lambda i: (i, 0))
    return pl.pallas_call(
        functools.partial(mixture_kernel, experts=experts, local=local),
        grid=(tokens // rows,),
        in_specs=[
            by_row(depth),
            by_row(units // 2),
            by_row(LANES),
            once(spot.shape),
            once((LANES, depth)),
            once((units, depth)),
        ],
        out_specs=[by_row(units), by_row(units // 2), by_row(LANES), by_row(depth)],
        out_shape=[
            jax.ShapeDtypeStruct((tokens, units), BF16),
            jax.ShapeDtypeStruct((tokens, units // 2), BF16),
            jax.ShapeDtypeStruct((tokens, LANES), BF16),
            jax.ShapeDtypeStruct((tokens, depth), BF16),
        ],
        compiler_params=pltpu.CompilerParams(vmem_limit_bytes=60 << 20),
        cost_estimate=pl.CostEstimate(
            flops=5 * tokens * depth * units, bytes_accessed=80 << 20, transcendentals=0
        ),
    )(mix, hidden_grad, kept, spot, router, weight)


def shards(
    layer_input,
    attention_gain,
    query_weight,
    key_weight,
    value_weight,
    query_bias,
    key_bias,
    value_bias,
    output_weight,
    mixture_gain,
    router_weight,
    expert_gate,
    expert_up,
    expert_down,
    shared_gate,
    shared_up,
    shared_down,
    shared_switch,
    slot_lengths,
    routes,
    cotangent,
):
    rows, depth = layer_input.shape[1:]
    groups = lax.axis_size("expert")
    tensors = lax.axis_size("tensor")
    slots = lax.axis_size("dp")
    slot_at = lax.axis_index("dp")
    block_at = lax.axis_index("expert")
    tensor_at = lax.axis_index("tensor")
    experts = router_weight.shape[1]
    local, _, expert_units = expert_gate.shape
    shared_units = shared_gate.shape[1] // groups
    capacity = rows * TOP // experts
    score_scale = HD ** (-0.5)
    heads_here = query_weight.shape[1] // HD
    wide = heads_here * HD
    piece = rows // tensors
    width = up_to(max(expert_units, shared_units), LANES)
    pair = 2 * width
    steps = local + 1
    length = slot_lengths[0]
    positions = block_at * rows + jnp.arange(rows, dtype=jnp.int32)
    live_rows = positions < length
    place = jnp.stack([block_at.astype(jnp.int32), length])

    links = Links()
    order = reversed_order(groups)
    behind = [(tensor_at - k) % tensors for k in range(tensors)]
    ahead = [(tensor_at + k) % tensors for k in range(tensors)]

    def rows_of(value, index):
        return rows_at(value, index * piece, piece)

    qkv_full = lax.all_gather(
        jnp.concatenate([query_weight, key_weight, value_weight], axis=1),
        ("dp", "expert"), axis=0, tiled=True,
    )
    inputs = layer_input[0].astype(F32)
    gain_one = attention_gain.astype(F32)
    inverse_one = lax.rsqrt(jnp.mean(inputs * inputs, axis=1, keepdims=True) + EPS)
    normed = (inputs * inverse_one * gain_one).astype(BF16)
    bias = jnp.concatenate([query_bias, key_bias, value_bias])[None, :]
    cosine_table, sine_table = rotary_tables(positions, HD)
    queries, kv_own = project(normed, qkv_full, bias, cosine_table, sine_table)
    kv = lax.all_gather(kv_own, "expert", axis=0, tiled=True)
    output_here = lax.all_gather(
        after(output_weight, kv), ("dp", "expert"), axis=0, tiled=True
    )

    (
        route_block, upstream_source, gate_source, up_source, down_source, shared_source, small_source,
    ) = after(
        (
            routes[0], cotangent[0], expert_gate, expert_up, expert_down,
            (shared_gate, shared_up, shared_down), (router_weight, shared_switch),
        ),
        kv_own,
    )

    shared_own = jnp.stack([w.T for w in shared_source])
    own_rows = shared_own.shape[2]

    def units_of(block):
        return lax.dynamic_slice_in_dim(shared_own, block * shared_units, shared_units, axis=1)

    shared_pieces = links.swaps([after(units_of(block_at ^ s), kv) for s in range(1, groups)], "expert")

    heads_low, log_sums = attend(place, queries, kv, heads_here, score_scale)

    expert_ids = jnp.arange(experts, dtype=jnp.int32)
    chosen = jnp.any(route_block[:, :, None] == expert_ids[None, None, :], axis=1) & live_rows[:, None]
    row_ids = jnp.arange(rows, dtype=jnp.int32)
    earlier = (row_ids[None, :] < row_ids[:, None]).astype(BF16)
    before = dot(earlier, chosen.astype(BF16))
    kept = chosen & (before < capacity)
    kept = jnp.pad(kept.astype(BF16), ((0, 0), (0, LANES - experts)))

    upstream_low = jnp.where(live_rows[:, None], upstream_source, jnp.zeros((), BF16))
    upstream_all = links.spread(upstream_low, "expert", low=2)
    kept_all = links.spread(kept, "expert", low=2)

    def pad_units(weight):
        return jnp.pad(weight, ((0, width - weight.shape[0]), (0, 0)))

    gates_t, ups_t, downs_t = (w.transpose(0, 2, 1) for w in (gate_source, up_source, down_source))
    weight_parts = []
    for j in range(local):
        weight_parts += [pad_units(gates_t[j]), pad_units(ups_t[j])]
    lin_weight = jnp.concatenate(weight_parts + [jnp.zeros((pair, depth), BF16)], axis=0)
    down_weight = jnp.concatenate(
        [pad_units(downs_t[j]) for j in range(local)] + [jnp.zeros((width, depth), BF16)], axis=0
    )
    small_weight = jnp.pad(
        jnp.concatenate([small_source[0].T, small_source[1][None, :]], axis=0),
        ((0, LANES - experts - 1), (0, 0)),
    )
    spot_at = jnp.concatenate(
        [block_at * local + jnp.arange(local, dtype=jnp.int32), jnp.full((1,), experts, jnp.int32)]
    )
    spot = (spot_at[:, None] == jnp.arange(LANES, dtype=jnp.int32)[None, :]).astype(F32)
    spot = jnp.pad(spot, ((0, up_to(steps, 8) - steps), (0, 0)))

    shared_pieces = [units_of(block_at)] + shared_pieces
    attended_part = dot_tt(after(heads_low, tuple(shared_pieces)), output_here).astype(BF16)
    shared_half = in_order(shared_pieces, [block_at ^ s for s in range(groups)], 2)
    halves = [shared_half] + links.shifts([shared_half] * (slots - 1), "dp")
    attended = lax.psum_scatter(attended_part, "tensor", scatter_dimension=0, tiled=True).astype(F32)
    inputs_own = rows_of(inputs, tensor_at)
    live_own = rows_of(live_rows, tensor_at)[:, None]
    residual = inputs_own + after(attended, (tuple(halves), upstream_all, kept_all))
    gain_two = mixture_gain.astype(F32)
    inverse_two = lax.rsqrt(jnp.mean(residual * residual, axis=1, keepdims=True) + EPS)
    mix_own = (residual * inverse_two * gain_two).astype(BF16)

    mix_all = lax.all_gather(mix_own, ("expert", "tensor"), axis=0, tiled=True)

    def all_blocks(half):
        found = jnp.concatenate([half, links.swap(half, "expert", 1)], axis=0)
        return in_order(
            [found[i * rows : (i + 1) * rows] for i in range(groups)], [block_at ^ s for s in order], 0
        )

    upstream_all, kept_all = (all_blocks(v) for v in after((upstream_all, kept_all), mix_own))

    halves = list(after(tuple(halves), mix_own))
    for k, found in enumerate(halves):
        column = (slot_at - k) % slots * (depth // slots)
        down_weight = lax.dynamic_update_slice(down_weight, found[2], (local * width, column))
        for i in (0, 1):
            lin_weight = lax.dynamic_update_slice(
                lin_weight, found[i], (local * pair + i * width, column)
            )
    hidden_grads = dot_tt(upstream_all, down_weight)

    lin_grads, hiddens, smalls, mix_part = mixture(
        after(mix_all, hidden_grads), hidden_grads, kept_all, spot, small_weight, lin_weight,
        rows, experts, local,
    )
    mix_sum = lax.psum_scatter(mix_part, ("expert", "tensor"), scatter_dimension=0, tiled=True)

    expert_rows = local * width
    down_grad = dot_nt(hiddens[:, :expert_rows], upstream_all).astype(BF16)

    def over_slots(part):
        return links.shifts([part] * (slots - 1), "dp")

    def total(own, arrived):
        return sum((a.astype(F32) for a in arrived), own.astype(F32))

    everyone = ("expert", "dp", "tensor")
    down_parts = jnp.concatenate(
        [down_grad[j * width : j * width + expert_units] for j in range(local)], axis=0
    )
    down_arrived = over_slots(down_parts)

    shared_lin_grad = dot_nt(lin_grads[:, local * pair :], mix_all).astype(BF16)
    shared_down_grad = dot_nt(hiddens[:, expert_rows:], after(upstream_all, down_parts)).astype(BF16)
    shared_part = jnp.concatenate(
        [
            shared_lin_grad[:shared_units],
            shared_lin_grad[width : width + shared_units],
            shared_down_grad[:shared_units],
        ],
        axis=0,
    )
    half = depth // slots

    def half_of(value, index):
        return lax.dynamic_slice_in_dim(value, index * half, half, axis=1)

    lin_parts = []
    for j in range(local):
        earlier_ones = (shared_part, tuple(down_arrived)) if j == local - 1 else (shared_part,)
        found = dot_nt(after(lin_grads[:, j * pair : (j + 1) * pair], earlier_ones), mix_all)
        found = found.astype(BF16)
        lin_parts.append(
            jnp.concatenate([found[:expert_units], found[width : width + expert_units]], axis=0)
        )
    shared_arrived = links.shifts(
        [half_of(shared_part, (slot_at + k) % slots) for k in range(1, slots)], "dp"
    )
    lin_arrived = [over_slots(part) for part in lin_parts]
    small_grad = dot_nt(after(smalls, down_parts), mix_all)[: experts + 1]

    output_part = dot(after(hiddens, down_parts), down_weight).astype(BF16)
    output_part = output_part.reshape(groups, rows, depth)

    output_part = links.scatter(output_part, "expert", 1, 2)
    mix_sum, output_part, lin_parts, shared_own_part = together(
        after(mix_sum, small_grad), output_part, tuple(lin_parts), shared_part
    )
    mix_grad = mix_sum.astype(F32)
    down_total = total(down_parts, after(tuple(down_arrived), mix_sum))
    down_total = down_total.reshape(local, expert_units, depth)
    scaled_two = mix_grad * gain_two
    mixture_gain_grad = jnp.sum(mix_grad * residual * inverse_two, axis=0)
    upstream_own = rows_of(upstream_low, tensor_at).astype(F32)
    residual_grad = (
        upstream_own
        + inverse_two * scaled_two
        - residual * inverse_two**3 * jnp.mean(scaled_two * residual, axis=1, keepdims=True)
    )
    attended_grad = residual_grad.astype(BF16)
    attended_all = lax.all_gather(attended_grad, "tensor", axis=0, tiled=True)
    output_part = links.scatter(output_part, "expert", 2, groups)[0]
    attended_all, output_part = together(after(attended_all, tuple(shared_arrived)), output_part)
    heads_grad = dot(attended_all, output_here).astype(BF16)

    mine = [rows_of(output_part, tensor_at)] + links.shifts(
        [rows_of(output_part, ahead[k]) for k in range(1, tensors)], "tensor"
    )
    query_grads, kv_grads = attend_back(
        place, queries, heads_grad, heads_low, log_sums, kv, heads_here, score_scale
    )
    kv_sum = lax.psum_scatter(kv_grads, "expert", scatter_dimension=0, tiled=True)
    pre_grad, bias_grad = turn_back(
        query_grads, after(kv_sum, tuple(mine)), cosine_table, sine_table)
    normed_part = dot_tt(pre_grad, qkv_full).astype(BF16)
    normed_sum = lax.psum_scatter(normed_part, "tensor", scatter_dimension=0, tiled=True)
    shared_sum = total(half_of(shared_own_part, slot_at), after(tuple(shared_arrived), pre_grad))
    shared_sum = shared_sum.astype(BF16).reshape(3, shared_units, depth // slots)
    def owned_by(block):
        return lax.dynamic_slice_in_dim(shared_sum, block * own_rows, own_rows, axis=2)

    shared_back = [owned_by(block_at)] + [
        links.swap(owned_by(block_at ^ s), "expert", s) for s in range(1, groups)
    ]
    normed_grad = after(normed_sum, tuple(shared_back[1:])).astype(F32)
    inverse_own = rows_of(inverse_one, tensor_at)
    scaled_one = normed_grad * gain_one
    attention_gain_grad = jnp.sum(normed_grad * inputs_own * inverse_own, axis=0)
    input_grad = (
        residual_grad
        + inverse_own * scaled_one
        - inputs_own * inverse_own**3 * jnp.mean(scaled_one * inputs_own, axis=1, keepdims=True)
    )
    input_low, pre_later = together(input_grad.astype(BF16), pre_grad)
    input_all = lax.all_gather(input_low, "tensor", axis=0, tiled=True)

    lin_total = jnp.stack(
        [
            total(part, after(tuple(found), input_low)).reshape(2, expert_units, depth)
            for part, found in zip(lin_parts, lin_arrived)
        ]
    )

    input_grad = input_all.astype(F32)
    own = depth // (slots * groups)

    def columns_for(value, part):
        return jnp.concatenate(
            [
                lax.dynamic_slice_in_dim(
                    value, (((slot_at + k) % slots) * groups + (block_at ^ s)) * own, own, axis=1
                )
                for s in part
                for k in range(slots)
            ],
            axis=1,
        )

    weight_grads = []
    for part in (order[: groups // 2], order[groups // 2 :]):
        weight_grads.append(
            jnp.concatenate(
                [
                    dot_nt(
                        columns_for(normed, part), after(pre_later, tuple(lin_arrived[0]))
                    ).astype(BF16),
                    dot_nt(columns_for(attended_all, part), heads_low).astype(BF16),
                ],
                axis=1,
            )
        )

    mixed = sum(s.astype(F32) for s in mine)
    output_own = jnp.where(live_own, residual + mixed, 0.0).astype(BF16)
    layer_output = lax.all_gather(after(output_own, input_all), "tensor", axis=0, tiled=True)

    shared_grads = side_by_side(place, shared_back)


    bias_place = lax.dynamic_update_slice_in_dim(
        jnp.zeros((tensors * 3 * wide,), F32), bias_grad[0], tensor_at * 3 * wide, axis=0
    )
    last_sums = sum_over_all(
        jnp.concatenate(
            [attention_gain_grad, mixture_gain_grad, small_grad.reshape(-1), bias_place]
        ),
        everyone,
    )
    weight_grad = links.meet(*weight_grads, "expert", 1)
    weight_grad = links.collect(*halves_of(weight_grad), "expert", low=2)
    weight_grads = [weight_grad[k * own : (k + 1) * own] for k in range(slots)]
    weight_grad = sum(
        p.astype(F32) for p in [weight_grads[0]] + links.shifts(weight_grads[1:], "dp")
    )

    small_total = last_sums[2 * depth : (3 + experts) * depth].reshape(experts + 1, depth)
    bias_total = lax.dynamic_slice_in_dim(
        last_sums, (3 + experts) * depth + tensor_at * 3 * wide, 3 * wide, axis=0
    )
    return (
        layer_output[None],
        input_grad[None],
        last_sums[:depth],
        weight_grad[:, :wide],
        weight_grad[:, wide : 2 * wide],
        weight_grad[:, 2 * wide : 3 * wide],
        bias_total[:wide],
        bias_total[wide : 2 * wide],
        bias_total[2 * wide :],
        weight_grad[:, 3 * wide :],
        last_sums[depth : 2 * depth],
        small_total[:experts].T,
        lin_total[:, 0].transpose(0, 2, 1),
        lin_total[:, 1].transpose(0, 2, 1),
        down_total.transpose(0, 2, 1),
        shared_grads[0],
        shared_grads[1],
        shared_grads[2],
        small_total[experts],
    )


def solution(mesh):
    dense = P(("dp", "expert"), "tensor")
    routed = P("expert", None, "tensor")
    rows = P("dp", "expert", None)
    in_specs = (
        rows, P(), dense, dense, dense, P("tensor"), P("tensor"), P("tensor"), dense, P(), P(),
        routed, routed, routed, dense, dense, dense, P(), P("dp"), rows, rows,
    )
    out_specs = (
        rows, rows, P(), dense, dense, dense, P("tensor"), P("tensor"), P("tensor"), dense, P(), P(),
        routed, routed, routed, dense, dense, dense, P(),
    )
    return jax.shard_map(shards, mesh=mesh, in_specs=in_specs, out_specs=out_specs, check_vma=False)
```

```python
import functools

import jax
import jax.numpy as jnp
from jax import lax
from jax.experimental import pallas as pl
from jax.experimental.pallas import tpu as pltpu
from jax.sharding import PartitionSpec as P

HD = 128
TOP = 4
LANES = 128

EPS = 1e-06
ROPE_BASE = 1000000.0
NEGATIVE = -1e30
F32 = jnp.float32
QUICK = pl.CostEstimate(flops=0, bytes_accessed=1 << 20, transcendentals=0)
BF16 = jnp.bfloat16


def up_to(value, multiple):
    return -(-value // multiple) * multiple


def rotary_tables(positions, head_size):
    half_size = head_size // 2
    exponent = 2.0 * jnp.arange(half_size, dtype=F32) / head_size
    inverse = ROPE_BASE ** (-exponent)
    angles = positions.astype(F32)[:, None] * inverse[None, :]
    cosine_half = jnp.cos(angles)
    sine_half = jnp.sin(angles)
    return (
        jnp.concatenate([cosine_half, cosine_half], axis=1),
        jnp.concatenate([-sine_half, sine_half], axis=1),
    )


class Links:
    def __init__(self):
        self.last = {}

    def send(self, link, values, axis, perms):
        before = None if link == "core" else self.last.get(link)
        if before is not None:
            tied = lax.optimization_barrier((tuple(values), before))
            values = tied[0]
        with jax.named_scope("over_" + link):
            arrived = tuple(lax.ppermute(v, axis, p) for v, p in zip(values, perms))
        self.last[link] = arrived
        return list(arrived)

    def swap(self, value, axis, bit):
        link = "x" if axis == "dp" else "core" if bit == 1 else "y"
        size = lax.axis_size(axis)
        return self.send(link, [value], axis, [[(i, i ^ bit) for i in range(size)]])[0]

    def swaps(self, values, axis):
        size = lax.axis_size(axis)
        perms = [[(i, i ^ s) for i in range(size)] for s in range(1, size)]
        return self.send("y", values, axis, perms)

    def shift(self, value, axis, by):
        size = lax.axis_size(axis)
        perm = [(i, (i + by) % size) for i in range(size)]
        return self.send("x" if axis == "dp" else "z", [value], axis, [perm])[0]

    def shifts(self, values, axis, direction=1):
        link = "x" if axis == "dp" else "z"
        size = lax.axis_size(axis)
        perms = [[(i, (i + direction * k) % size) for i in range(size)] for k in range(1, size)]
        return self.send(link, values, axis, perms[: len(values)])

    def spread(self, value, axis, low=1):
        bit = lax.axis_size(axis) // 2
        while bit >= low:
            value = jnp.concatenate([value, self.swap(value, axis, bit)], axis=0)
            bit //= 2
        return value

    def meet(self, near, far, axis, bit):
        arrived = self.swap(far, axis, bit)
        return (near.astype(F32) + arrived.astype(F32)).astype(near.dtype)

    def scatter(self, value, axis, bit, upto):
        at = lax.axis_index(axis)
        while bit < upto:
            value = value.reshape(value.shape[0] // 2, 2, *value.shape[1:])
            own = lax.rem(at // bit, 2)
            near, far = (
                lax.dynamic_index_in_dim(value, i, axis=1, keepdims=False) for i in (own, 1 - own)
            )
            value = self.meet(near, far, axis, bit)
            bit *= 2
        return value

    def collect(self, near, far, axis, low=1):
        bit = low
        while True:
            arrived = self.swap(far, axis, bit)
            near = (near.astype(F32) + arrived.astype(F32)).astype(near.dtype)
            bit *= 2
            if bit >= lax.axis_size(axis):
                return near
            half = near.shape[0] // 2
            near, far = near[:half], near[half:]


def sum_over_all(value, axes):
    for axis in axes:
        size = lax.axis_size(axis)
        bit = 1
        while bit < size:
            value = value + lax.ppermute(value, axis, [(i, i ^ bit) for i in range(size)])
            bit *= 2
    return value


def reversed_order(size):
    order, bit = [0], size // 2
    while bit:
        order = order + [i ^ bit for i in order]
        bit //= 2
    return order


def after(value, *others):
    return lax.optimization_barrier((value, others))[0]


def together(*values):
    return lax.optimization_barrier(values)


def halves_of(value):
    half = value.shape[0] // 2
    return value[:half], value[half:]


def rows_at(value, start, size):
    return lax.dynamic_slice_in_dim(value, start, size, axis=0)


def in_order(pieces, index, axis):
    size = pieces[0].shape[axis]
    shape = list(pieces[0].shape)
    shape[axis] = size * len(pieces)
    whole = jnp.zeros(shape, pieces[0].dtype)
    for piece, place in zip(pieces, index):
        whole = lax.dynamic_update_slice_in_dim(whole, piece, place * size, axis)
    return whole


def dot_tt(a, b):
    return lax.dot_general(a, b, (((1,), (1,)), ((), ())), preferred_element_type=F32)


def dot_nt(a, b):
    return lax.dot_general(a, b, (((0,), (0,)), ((), ())), preferred_element_type=F32)


def dot(a, b):
    return jnp.dot(a, b, preferred_element_type=F32)


def project_kernel(
    rows_ref, wq_ref, wk_ref, wv_ref, bq_ref, bk_ref, bv_ref, cosine_ref, sine_ref, q_ref, kv_ref
):
    source = rows_ref[...]
    cosine, sine = cosine_ref[...], sine_ref[...]

    def turned(value):
        return value * cosine + pltpu.roll(value, HD // 2, 1) * sine

    query = dot(source, wq_ref[...]) + bq_ref[...].astype(F32)
    key = dot(source, wk_ref[...]) + bk_ref[...].astype(F32)
    value = dot(source, wv_ref[...]) + bv_ref[...].astype(F32)
    for i in range(q_ref.shape[1] // HD):
        here = slice(i * HD, (i + 1) * HD)
        q_ref[:, here] = turned(query[:, here]).astype(BF16)
        kv_ref[:, 2 * i * HD : (2 * i + 1) * HD] = turned(key[:, here]).astype(BF16)
        kv_ref[:, (2 * i + 1) * HD : (2 * i + 2) * HD] = value[:, here].astype(BF16)


def project(source, weight, bias, cosine, sine):
    rows, depth = source.shape
    wide = weight.shape[1] // 3
    block = 2 * HD
    steps = wide // block
    whole = lambda shape: pl.BlockSpec(shape, lambda h: (0, 0))
    third = lambda size, i: pl.BlockSpec((size, block), lambda h: (0, i * steps + h))
    return pl.pallas_call(
        project_kernel,
        grid=(steps,),
        in_specs=[whole((rows, depth))]
        + [third(depth, i) for i in range(3)]
        + [third(1, i) for i in range(3)]
        + [whole((rows, HD))] * 2,
        out_specs=[
            pl.BlockSpec((rows, block), lambda h: (0, h)),
            pl.BlockSpec((rows, 2 * block), lambda h: (0, h)),
        ],
        out_shape=[
            jax.ShapeDtypeStruct((rows, wide), BF16),
            jax.ShapeDtypeStruct((rows, 2 * wide), BF16),
        ],
        compiler_params=pltpu.CompilerParams(vmem_limit_bytes=40 << 20),
        cost_estimate=QUICK,
    )(source, weight, weight, weight, bias, bias, bias, cosine, sine)


def turn_back_kernel(dq_ref, dkv_ref, cosine_ref, sine_ref, out_ref, sum_ref):
    cosine, sine = cosine_ref[...], sine_ref[...]
    wide = dq_ref.shape[1]

    def turned(value):
        return value * cosine - pltpu.roll(value, HD // 2, 1) * sine

    def store(at, value):
        low = value.astype(BF16)
        out_ref[:, at : at + HD] = low
        sum_ref[:, at : at + HD] = jnp.sum(low.astype(F32), axis=0, keepdims=True)

    for i in range(wide // HD):
        at = i * HD
        store(at, turned(dq_ref[:, at : at + HD]))
        here, there = slice(2 * at, 2 * at + HD), slice(2 * at + HD, 2 * at + 2 * HD)
        store(wide + at, turned(dkv_ref[:, here].astype(F32)))
        store(2 * wide + at, dkv_ref[:, there].astype(F32))


def turn_back(query_grads, kv_grads, cosine, sine):
    rows, wide = query_grads.shape
    return pl.pallas_call(
        turn_back_kernel,
        out_shape=[
            jax.ShapeDtypeStruct((rows, 3 * wide), BF16),
            jax.ShapeDtypeStruct((1, 3 * wide), F32),
        ],
        compiler_params=pltpu.CompilerParams(vmem_limit_bytes=40 << 20),
        cost_estimate=QUICK,
    )(query_grads, kv_grads, cosine, sine)


def seen_scores(query, key, length, score_scale):
    rows, columns = query.shape[0], key.shape[0]
    scores = dot_tt(query, key) * score_scale
    column = lax.broadcasted_iota(jnp.int32, (1, columns), 1)
    scores = scores + jnp.where(column < length, 0.0, NEGATIVE)
    far = lax.broadcasted_iota(jnp.int32, (rows, rows), 1) <= lax.broadcasted_iota(jnp.int32, (rows, rows), 0)
    near = jnp.where(far, scores[:, columns - rows :], NEGATIVE)
    return near if columns == rows else jnp.concatenate([scores[:, : columns - rows], near], axis=1)


def attend_kernel(place_ref, q_ref, kv_ref, out_ref, log_ref, *, groups, score_scale):
    me, length = place_ref[0], place_ref[1]
    rows = q_ref.shape[0]
    part = rows // 2

    def block(j):
        for first in range(0, rows, part):
            here, seen = slice(first, first + part), slice(0, j * rows + first + part)
            scores = seen_scores(q_ref[here, :], kv_ref[seen, :HD], length, score_scale)
            peak = jnp.max(scores, axis=1, keepdims=True)
            lifted = jnp.exp(scores - peak)
            total = jnp.sum(lifted, axis=1, keepdims=True)
            mix = dot(lifted.astype(BF16), kv_ref[seen, HD:])
            out_ref[here, :] = (mix / total).astype(BF16)
            log_ref[0, here, :] = peak + jnp.log(total)

    for j in range(groups):
        pl.when(me == j)(functools.partial(block, j))


def attend(place, query, kv, heads, score_scale):
    rows = query.shape[0]
    groups = kv.shape[0] // rows
    spec = pltpu.PrefetchScalarGridSpec(
        num_scalar_prefetch=1,
        grid=(heads,),
        in_specs=[
            pl.BlockSpec((rows, HD), lambda h, p: (0, h)),
            pl.BlockSpec((groups * rows, 2 * HD), lambda h, p: (0, h)),
        ],
        out_specs=[
            pl.BlockSpec((rows, HD), lambda h, p: (0, h)),
            pl.BlockSpec((1, rows, 1), lambda h, p: (h, 0, 0)),
        ],
    )
    work = heads * rows * rows * groups
    return pl.pallas_call(
        functools.partial(attend_kernel, groups=groups, score_scale=score_scale),
        grid_spec=spec,
        out_shape=[
            jax.ShapeDtypeStruct((rows, heads * HD), BF16),
            jax.ShapeDtypeStruct((heads, rows, 1), F32),
        ],
        compiler_params=pltpu.CompilerParams(vmem_limit_bytes=40 << 20),
        cost_estimate=QUICK,
    )(place, query, kv)


def attend_back_kernel(
    place_ref, q_ref, g_ref, o_ref, log_ref, kv_ref, dq_ref, dkv_ref, sums, *, groups, score_scale
):
    me, length = place_ref[0], place_ref[1]
    rows = q_ref.shape[0]
    part = rows // 2

    def block(j):
        for first in reversed(range(0, rows, part)):
            here, seen = slice(first, first + part), slice(0, j * rows + first + part)
            query, grad, key = q_ref[here, :], g_ref[here, :], kv_ref[seen, :HD]
            centre = jnp.sum(
                grad.astype(F32) * o_ref[here, :].astype(F32), axis=1, keepdims=True
            )
            scores = seen_scores(query, key, length, score_scale)
            weights = jnp.exp(scores - log_ref[0, here, :])
            weight_grad = dot_tt(grad, kv_ref[seen, HD:])
            score_grad = (weights * (weight_grad - centre)).astype(BF16)
            dq_ref[here, :] = dot(score_grad, key) * score_scale
            key_grad = dot_nt(score_grad, query) * score_scale
            value_grad = dot_nt(weights.astype(BF16), grad)
            if first + part == rows:
                sums[seen, :HD] = key_grad
                sums[seen, HD:] = value_grad
            else:
                sums[seen, :HD] += key_grad
                sums[seen, HD:] += value_grad
        dkv_ref[: (j + 1) * rows, :] = sums[: (j + 1) * rows, :].astype(BF16)
        if j + 1 < groups:
            rest = (groups - 1 - j) * rows
            dkv_ref[(j + 1) * rows :, :] = jnp.zeros((rest, 2 * HD), BF16)

    for j in range(groups):
        pl.when(me == j)(functools.partial(block, j))


def attend_back(place, query, grad, out, log_sums, kv, heads, score_scale):
    rows = query.shape[0]
    groups = kv.shape[0] // rows
    head = pl.BlockSpec((rows, HD), lambda h, p: (0, h))
    pair = pl.BlockSpec((groups * rows, 2 * HD), lambda h, p: (0, h))
    spec = pltpu.PrefetchScalarGridSpec(
        num_scalar_prefetch=1,
        grid=(heads,),
        in_specs=[head, head, head, pl.BlockSpec((1, rows, 1), lambda h, p: (h, 0, 0)), pair],
        out_specs=[head, pair],
        scratch_shapes=[pltpu.VMEM((groups * rows, 2 * HD), F32)],
    )
    work = heads * rows * rows * groups
    return pl.pallas_call(
        functools.partial(attend_back_kernel, groups=groups, score_scale=score_scale),
        grid_spec=spec,
        out_shape=[
            jax.ShapeDtypeStruct((rows, heads * HD), F32),
            jax.ShapeDtypeStruct((groups * rows, 2 * heads * HD), BF16),
        ],
        compiler_params=pltpu.CompilerParams(vmem_limit_bytes=48 << 20),
        cost_estimate=QUICK,
    )(place, query, grad, out, log_sums, kv)


def side_by_side_kernel(place_ref, *refs, groups):
    pieces, stack, outs = refs[:groups], refs[-1], refs[groups:-1]
    units = pieces[0].shape[1]
    for s in range(groups):
        stack[s] = pieces[s][...]
    for j in range(groups):
        found = stack[place_ref[0] ^ j]
        for i, out in enumerate(outs):
            out[:, j * units : (j + 1) * units] = found[i].astype(F32).T


def side_by_side(place, pieces):
    count, units, rows = pieces[0].shape
    groups = len(pieces)
    return pl.pallas_call(
        functools.partial(side_by_side_kernel, groups=groups),
        grid_spec=pltpu.PrefetchScalarGridSpec(
            num_scalar_prefetch=1,
            in_specs=[pl.BlockSpec(memory_space=pltpu.VMEM)] * groups,
            out_specs=[pl.BlockSpec(memory_space=pltpu.VMEM)] * count,
            scratch_shapes=[pltpu.VMEM((groups, count, units, rows), BF16)],
        ),
        out_shape=[jax.ShapeDtypeStruct((rows, groups * units), F32)] * count,
        compiler_params=pltpu.CompilerParams(vmem_limit_bytes=40 << 20),
    )(place, *pieces)


def mixture_kernel(
    mix_ref, hidden_grad_ref, kept_ref, spot_ref, router_ref, weight_ref,
    lin_grad_ref, hidden_ref, small_ref, part_ref, *, experts, local,
):
    pair = weight_ref.shape[0] // (local + 1)
    width = pair // 2
    mix = mix_ref[...]
    lane = lax.broadcasted_iota(jnp.int32, kept_ref.shape, 1)
    logits = dot_tt(mix, router_ref[...])
    masked = jnp.where(lane < experts, logits, NEGATIVE)
    lifted = jnp.exp(masked - jnp.max(masked, axis=1, keepdims=True))
    probs = lifted / jnp.sum(lifted, axis=1, keepdims=True)
    kept = kept_ref[...].astype(F32)
    grads = jnp.zeros(kept_ref.shape, F32)
    for step in range(local + 1):
        spot = spot_ref[step : step + 1, :]
        if step < local:
            factor = jnp.sum(kept * spot, axis=1, keepdims=True)
            scale = jnp.sum(probs * kept * spot, axis=1, keepdims=True)
        else:
            scale = jax.nn.sigmoid(jnp.sum(logits * spot, axis=1, keepdims=True))
            factor = scale * (1.0 - scale)
        at = step * pair
        lin = dot_tt(mix, weight_ref[at : at + pair, :])
        gate_lin, up_lin = lin[:, :width], lin[:, width:]
        logistic = jax.nn.sigmoid(gate_lin)
        silu = gate_lin * logistic
        hidden = silu * up_lin
        hidden_grad = hidden_grad_ref[:, step * width : (step + 1) * width]
        row_sum = jnp.sum(hidden * hidden_grad, axis=1, keepdims=True)
        grads += row_sum * factor * spot
        hidden_ref[:, step * width : (step + 1) * width] = (scale * hidden).astype(BF16)
        scaled = scale * hidden_grad
        lin_grad_ref[:, at : at + width] = (
            scaled * up_lin * (logistic + silu * (1.0 - logistic))
        ).astype(BF16)
        lin_grad_ref[:, at + width : at + pair] = (scaled * silu).astype(BF16)
    routed_grads = jnp.where(lane < experts, grads, 0.0)
    inner = jnp.sum(probs * routed_grads, axis=1, keepdims=True)
    small = jnp.where(lane < experts, probs * (grads - inner), grads).astype(BF16)
    small_ref[...] = small
    part_ref[...] = (
        dot(lin_grad_ref[...], weight_ref[...]) + dot(small, router_ref[...])
    ).astype(BF16)


def mixture(mix, hidden_grad, kept, spot, router, weight, rows, experts, local):
    tokens, depth = mix.shape
    units = weight.shape[0]
    once = lambda shape: pl.BlockSpec(shape, lambda i: (0, 0), pipeline_mode=pl.Buffered(1))
    by_row = lambda size: pl.BlockSpec((rows, size), lambda i: (i, 0))
    return pl.pallas_call(
        functools.partial(mixture_kernel, experts=experts, local=local),
        grid=(tokens // rows,),
        in_specs=[
            by_row(depth),
            by_row(units // 2),
            by_row(LANES),
            once(spot.shape),
            once((LANES, depth)),
            once((units, depth)),
        ],
        out_specs=[by_row(units), by_row(units // 2), by_row(LANES), by_row(depth)],
        out_shape=[
            jax.ShapeDtypeStruct((tokens, units), BF16),
            jax.ShapeDtypeStruct((tokens, units // 2), BF16),
            jax.ShapeDtypeStruct((tokens, LANES), BF16),
            jax.ShapeDtypeStruct((tokens, depth), BF16),
        ],
        compiler_params=pltpu.CompilerParams(vmem_limit_bytes=60 << 20),
        cost_estimate=pl.CostEstimate(
            flops=5 * tokens * depth * units, bytes_accessed=80 << 20, transcendentals=0
        ),
    )(mix, hidden_grad, kept, spot, router, weight)


def shards(
    layer_input,
    attention_gain,
    query_weight,
    key_weight,
    value_weight,
    query_bias,
    key_bias,
    value_bias,
    output_weight,
    mixture_gain,
    router_weight,
    expert_gate,
    expert_up,
    expert_down,
    shared_gate,
    shared_up,
    shared_down,
    shared_switch,
    slot_lengths,
    routes,
    cotangent,
):
    rows, depth = layer_input.shape[1:]
    groups = lax.axis_size("expert")
    tensors = lax.axis_size("tensor")
    slots = lax.axis_size("dp")
    slot_at = lax.axis_index("dp")
    block_at = lax.axis_index("expert")
    tensor_at = lax.axis_index("tensor")
    experts = router_weight.shape[1]
    local, _, expert_units = expert_gate.shape
    shared_units = shared_gate.shape[1] // groups
    capacity = rows * TOP // experts
    score_scale = HD ** (-0.5)
    heads_here = query_weight.shape[1] // HD
    wide = heads_here * HD
    piece = rows // tensors
    width = up_to(max(expert_units, shared_units), LANES)
    pair = 2 * width
    steps = local + 1
    length = slot_lengths[0]
    positions = block_at * rows + jnp.arange(rows, dtype=jnp.int32)
    live_rows = positions < length
    place = jnp.stack([block_at.astype(jnp.int32), length])

    links = Links()
    order = reversed_order(groups)
    behind = [(tensor_at - k) % tensors for k in range(tensors)]
    ahead = [(tensor_at + k) % tensors for k in range(tensors)]

    def rows_of(value, index):
        return rows_at(value, index * piece, piece)

    qkv_full = lax.all_gather(
        jnp.concatenate([query_weight, key_weight, value_weight], axis=1),
        ("dp", "expert"), axis=0, tiled=True,
    )
    inputs = layer_input[0].astype(F32)
    gain_one = attention_gain.astype(F32)
    inverse_one = lax.rsqrt(jnp.mean(inputs * inputs, axis=1, keepdims=True) + EPS)
    normed = (inputs * inverse_one * gain_one).astype(BF16)
    bias = jnp.concatenate([query_bias, key_bias, value_bias])[None, :]
    cosine_table, sine_table = rotary_tables(positions, HD)
    queries, kv_own = project(normed, qkv_full, bias, cosine_table, sine_table)
    kv = lax.all_gather(kv_own, "expert", axis=0, tiled=True)
    output_here = lax.all_gather(
        after(output_weight, kv), ("dp", "expert"), axis=0, tiled=True
    )

    (
        route_block, upstream_source, gate_source, up_source, down_source, shared_source, small_source,
    ) = after(
        (
            routes[0], cotangent[0], expert_gate, expert_up, expert_down,
            (shared_gate, shared_up, shared_down), (router_weight, shared_switch),
        ),
        kv_own,
    )

    shared_own = jnp.stack([w.T for w in shared_source])
    own_rows = shared_own.shape[2]

    def units_of(block):
        return lax.dynamic_slice_in_dim(shared_own, block * shared_units, shared_units, axis=1)

    shared_pieces = links.swaps([after(units_of(block_at ^ s), kv) for s in range(1, groups)], "expert")

    heads_low, log_sums = attend(place, queries, kv, heads_here, score_scale)

    expert_ids = jnp.arange(experts, dtype=jnp.int32)
    chosen = jnp.any(route_block[:, :, None] == expert_ids[None, None, :], axis=1) & live_rows[:, None]
    row_ids = jnp.arange(rows, dtype=jnp.int32)
    earlier = (row_ids[None, :] < row_ids[:, None]).astype(BF16)
    before = dot(earlier, chosen.astype(BF16))
    kept = chosen & (before < capacity)
    kept = jnp.pad(kept.astype(BF16), ((0, 0), (0, LANES - experts)))

    upstream_low = jnp.where(live_rows[:, None], upstream_source, jnp.zeros((), BF16))
    shared_half = in_order(
        [units_of(block_at)] + shared_pieces, [block_at ^ s for s in range(groups)], 2
    )
    heads_ready, upstream_low, kept, shared_half = together(heads_low, upstream_low, kept, shared_half)
    kept_all = links.spread(kept, "expert", low=2)
    upstream_all = links.spread(upstream_low, "expert", low=2)

    def pad_units(weight):
        return jnp.pad(weight, ((0, width - weight.shape[0]), (0, 0)))

    gates_t, ups_t, downs_t = (w.transpose(0, 2, 1) for w in (gate_source, up_source, down_source))
    weight_parts = []
    for j in range(local):
        weight_parts += [pad_units(gates_t[j]), pad_units(ups_t[j])]
    lin_weight = jnp.concatenate(weight_parts + [jnp.zeros((pair, depth), BF16)], axis=0)
    down_weight = jnp.concatenate(
        [pad_units(downs_t[j]) for j in range(local)] + [jnp.zeros((width, depth), BF16)], axis=0
    )
    small_weight = jnp.pad(
        jnp.concatenate([small_source[0].T, small_source[1][None, :]], axis=0),
        ((0, LANES - experts - 1), (0, 0)),
    )
    spot_at = jnp.concatenate(
        [block_at * local + jnp.arange(local, dtype=jnp.int32), jnp.full((1,), experts, jnp.int32)]
    )
    spot = (spot_at[:, None] == jnp.arange(LANES, dtype=jnp.int32)[None, :]).astype(F32)
    spot = jnp.pad(spot, ((0, up_to(steps, 8) - steps), (0, 0)))

    attended_part = dot_tt(heads_ready, output_here).astype(BF16)
    halves = [shared_half] + links.shifts([shared_half] * (slots - 1), "dp")
    attended = lax.psum_scatter(attended_part, "tensor", scatter_dimension=0, tiled=True).astype(F32)
    inputs_own = rows_of(inputs, tensor_at)
    live_own = rows_of(live_rows, tensor_at)[:, None]
    residual = inputs_own + after(attended, (tuple(halves), upstream_all, kept_all))
    gain_two = mixture_gain.astype(F32)
    inverse_two = lax.rsqrt(jnp.mean(residual * residual, axis=1, keepdims=True) + EPS)
    mix_own = (residual * inverse_two * gain_two).astype(BF16)

    mix_all = lax.all_gather(mix_own, ("expert", "tensor"), axis=0, tiled=True)

    def all_blocks(half):
        found = jnp.concatenate([half, links.swap(half, "expert", 1)], axis=0)
        return in_order(
            [found[i * rows : (i + 1) * rows] for i in range(groups)], [block_at ^ s for s in order], 0
        )

    upstream_all, kept_all = (all_blocks(v) for v in after((upstream_all, kept_all), mix_own))

    halves = list(after(tuple(halves), mix_own))
    for k, found in enumerate(halves):
        column = (slot_at - k) % slots * (depth // slots)
        down_weight = lax.dynamic_update_slice(down_weight, found[2], (local * width, column))
        for i in (0, 1):
            lin_weight = lax.dynamic_update_slice(
                lin_weight, found[i], (local * pair + i * width, column)
            )
    hidden_grads = dot_tt(upstream_all, down_weight)

    lin_grads, hiddens, smalls, mix_part = mixture(
        after(mix_all, hidden_grads), hidden_grads, kept_all, spot, small_weight, lin_weight,
        rows, experts, local,
    )
    mix_sum = lax.psum_scatter(mix_part, ("expert", "tensor"), scatter_dimension=0, tiled=True)

    expert_rows = local * width
    down_grad = dot_nt(hiddens[:, :expert_rows], upstream_all).astype(BF16)

    def over_slots(part):
        return links.shifts([part] * (slots - 1), "dp")

    def total(own, arrived):
        return sum((a.astype(F32) for a in arrived), own.astype(F32))

    everyone = ("expert", "dp", "tensor")
    down_parts = jnp.concatenate(
        [down_grad[j * width : j * width + expert_units] for j in range(local)], axis=0
    )
    down_arrived = over_slots(down_parts)

    shared_lin_grad = dot_nt(lin_grads[:, local * pair :], mix_all).astype(BF16)
    shared_down_grad = dot_nt(hiddens[:, expert_rows:], after(upstream_all, down_parts)).astype(BF16)
    shared_part = jnp.concatenate(
        [
            shared_lin_grad[:shared_units],
            shared_lin_grad[width : width + shared_units],
            shared_down_grad[:shared_units],
        ],
        axis=0,
    )
    half = depth // slots

    def half_of(value, index):
        return lax.dynamic_slice_in_dim(value, index * half, half, axis=1)

    lin_parts = []
    for j in range(local):
        earlier_ones = (shared_part, tuple(down_arrived)) if j == local - 1 else (shared_part,)
        found = dot_nt(after(lin_grads[:, j * pair : (j + 1) * pair], earlier_ones), mix_all)
        found = found.astype(BF16)
        lin_parts.append(
            jnp.concatenate([found[:expert_units], found[width : width + expert_units]], axis=0)
        )
    shared_arrived = links.shifts(
        [half_of(shared_part, (slot_at + k) % slots) for k in range(1, slots)], "dp"
    )
    lin_arrived = [over_slots(part) for part in lin_parts]
    small_grad = dot_nt(after(smalls, down_parts), mix_all)[: experts + 1]

    output_part = dot(after(hiddens, down_parts), down_weight).astype(BF16)
    output_part = output_part.reshape(groups, rows, depth)

    output_part = links.scatter(output_part, "expert", 1, 2)
    mix_sum, output_part, lin_parts, shared_own_part = together(
        after(mix_sum, small_grad), output_part, tuple(lin_parts), shared_part
    )
    mix_grad = mix_sum.astype(F32)
    down_total = total(down_parts, after(tuple(down_arrived), mix_sum))
    down_total = down_total.reshape(local, expert_units, depth)
    scaled_two = mix_grad * gain_two
    mixture_gain_grad = jnp.sum(mix_grad * residual * inverse_two, axis=0)
    upstream_own = rows_of(upstream_low, tensor_at).astype(F32)
    residual_grad = (
        upstream_own
        + inverse_two * scaled_two
        - residual * inverse_two**3 * jnp.mean(scaled_two * residual, axis=1, keepdims=True)
    )
    attended_grad = residual_grad.astype(BF16)
    attended_all = lax.all_gather(attended_grad, "tensor", axis=0, tiled=True)
    output_part = links.scatter(output_part, "expert", 2, groups)[0]
    attended_all, output_part = together(after(attended_all, tuple(shared_arrived)), output_part)
    heads_grad = dot(attended_all, output_here).astype(BF16)

    mine = [rows_of(output_part, tensor_at)] + links.shifts(
        [rows_of(output_part, ahead[k]) for k in range(1, tensors)], "tensor"
    )
    query_grads, kv_grads = attend_back(
        place, queries, heads_grad, heads_low, log_sums, kv, heads_here, score_scale
    )
    kv_sum = lax.psum_scatter(kv_grads, "expert", scatter_dimension=0, tiled=True)
    pre_grad, bias_grad = turn_back(
        query_grads, after(kv_sum, tuple(mine)), cosine_table, sine_table)
    normed_part = dot_tt(pre_grad, qkv_full).astype(BF16)
    normed_sum = lax.psum_scatter(normed_part, "tensor", scatter_dimension=0, tiled=True)
    shared_sum = total(half_of(shared_own_part, slot_at), after(tuple(shared_arrived), pre_grad))
    shared_sum = shared_sum.astype(BF16).reshape(3, shared_units, depth // slots)
    def owned_by(block):
        return lax.dynamic_slice_in_dim(shared_sum, block * own_rows, own_rows, axis=2)

    shared_back = [owned_by(block_at)] + [
        links.swap(owned_by(block_at ^ s), "expert", s) for s in range(1, groups)
    ]
    normed_grad = after(normed_sum, tuple(shared_back[1:])).astype(F32)
    inverse_own = rows_of(inverse_one, tensor_at)
    scaled_one = normed_grad * gain_one
    attention_gain_grad = jnp.sum(normed_grad * inputs_own * inverse_own, axis=0)
    input_grad = (
        residual_grad
        + inverse_own * scaled_one
        - inputs_own * inverse_own**3 * jnp.mean(scaled_one * inputs_own, axis=1, keepdims=True)
    )
    input_low, pre_later = together(input_grad.astype(BF16), pre_grad)
    input_all = lax.all_gather(input_low, "tensor", axis=0, tiled=True)

    lin_total = jnp.stack(
        [
            total(part, after(tuple(found), input_low)).reshape(2, expert_units, depth)
            for part, found in zip(lin_parts, lin_arrived)
        ]
    )

    input_grad = input_all.astype(F32)
    own = depth // (slots * groups)

    def columns_for(value, part):
        return jnp.concatenate(
            [
                lax.dynamic_slice_in_dim(
                    value, (((slot_at + k) % slots) * groups + (block_at ^ s)) * own, own, axis=1
                )
                for s in part
                for k in range(slots)
            ],
            axis=1,
        )

    weight_grads = []
    for part in (order[: groups // 2], order[groups // 2 :]):
        weight_grads.append(
            jnp.concatenate(
                [
                    dot_nt(
                        columns_for(normed, part), after(pre_later, tuple(lin_arrived[0]))
                    ).astype(BF16),
                    dot_nt(columns_for(attended_all, part), heads_low).astype(BF16),
                ],
                axis=1,
            )
        )

    mixed = sum(s.astype(F32) for s in mine)
    output_own = jnp.where(live_own, residual + mixed, 0.0).astype(BF16)
    layer_output = lax.all_gather(after(output_own, input_all), "tensor", axis=0, tiled=True)

    shared_grads = side_by_side(place, shared_back)


    bias_place = lax.dynamic_update_slice_in_dim(
        jnp.zeros((tensors * 3 * wide,), F32), bias_grad[0], tensor_at * 3 * wide, axis=0
    )
    last_sums = sum_over_all(
        jnp.concatenate(
            [attention_gain_grad, mixture_gain_grad, small_grad.reshape(-1), bias_place]
        ),
        everyone,
    )
    weight_grad = links.meet(*weight_grads, "expert", 1)
    weight_grad = links.collect(*halves_of(weight_grad), "expert", low=2)
    weight_grads = [weight_grad[k * own : (k + 1) * own] for k in range(slots)]
    weight_grad = sum(
        p.astype(F32) for p in [weight_grads[0]] + links.shifts(weight_grads[1:], "dp")
    )

    small_total = last_sums[2 * depth : (3 + experts) * depth].reshape(experts + 1, depth)
    bias_total = lax.dynamic_slice_in_dim(
        last_sums, (3 + experts) * depth + tensor_at * 3 * wide, 3 * wide, axis=0
    )
    return (
        layer_output[None],
        input_grad[None],
        last_sums[:depth],
        weight_grad[:, :wide],
        weight_grad[:, wide : 2 * wide],
        weight_grad[:, 2 * wide : 3 * wide],
        bias_total[:wide],
        bias_total[wide : 2 * wide],
        bias_total[2 * wide :],
        weight_grad[:, 3 * wide :],
        last_sums[depth : 2 * depth],
        small_total[:experts].T,
        lin_total[:, 0].transpose(0, 2, 1),
        lin_total[:, 1].transpose(0, 2, 1),
        down_total.transpose(0, 2, 1),
        shared_grads[0],
        shared_grads[1],
        shared_grads[2],
        small_total[experts],
    )


def solution(mesh):
    dense = P(("dp", "expert"), "tensor")
    routed = P("expert", None, "tensor")
    rows = P("dp", "expert", None)
    in_specs = (
        rows, P(), dense, dense, dense, P("tensor"), P("tensor"), P("tensor"), dense, P(), P(),
        routed, routed, routed, dense, dense, dense, P(), P("dp"), rows, rows,
    )
    out_specs = (
        rows, rows, P(), dense, dense, dense, P("tensor"), P("tensor"), P("tensor"), dense, P(), P(),
        routed, routed, routed, dense, dense, dense, P(),
    )
    return jax.shard_map(shards, mesh=mesh, in_specs=in_specs, out_specs=out_specs, check_vma=False)
```
